512 devices in a mesh: ctx: 64 (over y_lo, z, x), tp: 8 (over y_hi, core).
Axes of the slice: x: 4, y: 8 (y_hi: 4, y_lo: 2; y = y_hi * 2 + y_lo), z: 8, core: 2. Of those that a mesh axis runs over, the one named last changes fastest.
Arguments:
- queries: bfloat16 [16384, 8192], P('ctx', 'tp'), may hold values from -128 to 128
- cotangent: bfloat16 [16384, 8192], P('ctx', 'tp'), may hold values from -96 to 96
- image_keys: bfloat16 [64, 64, 1024], P('ctx', None, 'tp'), may hold values from -8 to 8
- image_values: bfloat16 [64, 64, 1024], P('ctx', None, 'tp'), may hold values from -6 to 6
- attn_gate: float32 [1], replicated, may hold values from 0.4 to 1.5
- block_mask: int32 [128, 64], P('ctx'), may hold values from 0 to 1, as said below
- image_owner: int32 [64], replicated, may hold values from 0 to 63, each once
Outputs:
- query_grad: bfloat16 [16384, 8192], P('ctx', 'tp')
- key_grad: bfloat16 [64, 64, 1024], P('ctx', None, 'tp')
- value_grad: bfloat16 [64, 64, 1024], P('ctx', None, 'tp')
- gate_grad: float32 [1], replicated
The draws below stay inside these ranges and needn't reach their ends.
Inputs may be any that keep to these rules, and one draw needn't show every extreme that they name: `block_mask`: every text block reads at least one image; the 2 blocks of one index of ctx together read exactly 32 distinct images.
All inputs are finite; a program needn't handle non-finite values.
Results may differ from the reference program's by a relative error of at most 0.02.
Values may be sent and summed in bfloat16 or wider, within the bound.
A program may use at most 64 MiB of HBM per device.

```python
import math
import jax
import jax.numpy as jnp
from jax import lax

H = 64
KVH = 8
HD = 128
TOK_DEV = 256
BLK = 128
IMG_TOK = 64
NIMG = 64
RMAX = 32
TEXT = 16384
NBLK = 128
BLK_DEV = 2
N_CTX = 64


def draw_queries(key, part):
    entries = jax.random.normal(jax.random.fold_in(key, 1), (TEXT, H * HD), jnp.float32)
    return entries.astype(jnp.bfloat16)


def draw_image_keys(key, part):
    entries = jax.random.normal(jax.random.fold_in(key, 3), (NIMG, IMG_TOK, KVH * HD), jnp.float32)
    return entries.astype(jnp.bfloat16)


def draw_block_mask(key, part):
    shards = NBLK // BLK_DEV
    key_perm, key_bits = jax.random.split(key, 2)
    orders = jax.vmap(lambda subkey: jax.random.permutation(subkey, NIMG))(jax.random.split(key_perm, shards))
    positions = jnp.argsort(orders, axis=1)
    coin_flips = jax.random.randint(key_bits, (shards, BLK_DEV, NIMG), 0, 2)
    block_index = jnp.arange(BLK_DEV)[None, :, None]
    position_grid = positions[:, None, :]
    chosen = position_grid < RMAX
    reading = chosen & ((position_grid % BLK_DEV == block_index) | (position_grid == 0) | (coin_flips == 1))
    return reading.astype(jnp.int32).reshape(NBLK, NIMG)


def steps_of(stream_key, extent, pieces, least, top_value):
    level, own = 1.0, jax.random.fold_in(stream_key, 6)
    for position, shards_of in pieces:
        draws = jnp.exp(jax.random.uniform(jax.random.fold_in(own, position), (shards_of,), jnp.float32, least / len(pieces), top_value / len(pieces)))
        level = level * jnp.repeat(draws, extent[position] // shards_of).reshape([-1 if axis == position else 1 for axis in range(len(extent))])
    return level


def noise(stream_key, shape, spread, reach, cuts=(), kind=jnp.bfloat16):
    factor_of = steps_of(stream_key, shape, cuts, -0.22, 0.18) if cuts else 1.0
    result = jax.random.normal(stream_key, shape, jnp.float32) * spread * factor_of
    return jnp.minimum(jnp.maximum(result, -reach), reach).astype(kind)


def setup_inputs(seed: int = 0) -> dict:
    streams_of = jax.random.split(jax.random.key(seed), 8)
    queries = draw_queries(jax.random.fold_in(streams_of[7], 71), 0)
    cotangent = noise(streams_of[1], (TEXT, H * HD), 16.0, 96.0, ((0, 64), (1, 8)))
    image_keys = draw_image_keys(jax.random.fold_in(streams_of[7], 71), 0)
    image_values = noise(streams_of[3], (NIMG, IMG_TOK, KVH * HD), 1.0, 6.0, ((0, 64), (2, 8)))
    attn_gate = jnp.clip(jax.random.uniform(streams_of[4], (1,), jnp.float32, 0.4, 1.5), 0.4, 1.5)
    block_mask = draw_block_mask(jax.random.fold_in(streams_of[7], 71), 0)
    image_owner = jax.random.permutation(streams_of[6], NIMG).astype(jnp.int32)
    return dict(queries=queries, cotangent=cotangent, image_keys=image_keys, image_values=image_values, attn_gate=attn_gate, block_mask=block_mask, image_owner=image_owner)


def select_images(mask_rows, image_owner):
    read_any = lax.optimization_barrier(jnp.max(mask_rows, axis=0))
    ranking = read_any * (2 * NIMG) + (NIMG - 1 - jnp.arange(NIMG, dtype=jnp.int32))
    top_vals, image_ids = lax.top_k(ranking, RMAX)
    image_ids = image_ids.astype(jnp.int32)
    is_read = read_any[image_ids] > 0
    slot_ids = image_owner[image_ids].astype(jnp.int32)
    block_keep = (mask_rows[:, image_ids] > 0) & is_read[None, :]
    keep_mask = jnp.repeat(jnp.repeat(block_keep, BLK, axis=0), IMG_TOK, axis=1)
    return (slot_ids, is_read, keep_mask)

def group_backward(query_rows, cot_rows, key_rows, value_rows, keep_mask, gate_value):
    groups = H // KVH
    inv_root = 1.0 / math.sqrt(HD)
    query_f = query_rows.reshape(TOK_DEV, KVH, groups, HD).astype(jnp.float32)
    key_f = key_rows.reshape(RMAX * IMG_TOK, KVH, HD).astype(jnp.float32)
    value_f = value_rows.reshape(RMAX * IMG_TOK, KVH, HD).astype(jnp.float32)
    scores = jnp.einsum('tkgd,skd->kgts', query_f, key_f) * inv_root
    scores = jnp.where(keep_mask, scores, -1e+30)
    row_max = lax.optimization_barrier(jnp.max(scores, axis=-1, keepdims=True))
    exp_terms = jnp.where(keep_mask, jnp.exp(scores - row_max), 0.0)
    prob_full = exp_terms / lax.optimization_barrier(jnp.sum(exp_terms, axis=-1, keepdims=True))
    prob_half = prob_full.astype(jnp.bfloat16)
    attended = jnp.einsum('kgts,skd->tkgd', prob_half.astype(jnp.float32), value_f)
    cot_f = cot_rows.reshape(TOK_DEV, KVH, groups, HD).astype(jnp.float32)
    gate_part = jnp.sum(cot_f * attended)
    attn_grad = (gate_value * cot_f).astype(jnp.bfloat16)
    grad_f = attn_grad.astype(jnp.float32)
    prob_grad = jnp.einsum('tkgd,skd->kgts', grad_f, value_f)
    row_delta = jnp.einsum('tkgd,tkgd->kgt', grad_f, attended)
    score_grad = (prob_full * (prob_grad - row_delta[..., None]) * inv_root).astype(jnp.bfloat16)
    score_f = score_grad.astype(jnp.float32)
    query_grad = jnp.einsum('kgts,skd->tkgd', score_f, key_f).astype(jnp.bfloat16)
    key_grad = jnp.einsum('kgts,tkgd->skd', score_f, query_f)
    value_grad = jnp.einsum('kgts,tkgd->skd', prob_half.astype(jnp.float32), grad_f)
    return (query_grad.reshape(TOK_DEV, H * HD), key_grad, value_grad, gate_part)

def reference(queries, cotangent, image_keys, image_values, attn_gate, block_mask, image_owner):
    gate_value = jnp.tanh(attn_gate[0])
    query_groups = queries.reshape(N_CTX, TOK_DEV, H * HD)
    cot_groups = cotangent.reshape(N_CTX, TOK_DEV, H * HD)
    mask_groups = block_mask.reshape(N_CTX, BLK_DEV, NIMG)

    def group_step(state_in, group_inputs):
        grads_acc, gate_acc = state_in
        query_rows, cot_rows, mask_rows = group_inputs
        slot_ids, is_read, keep_mask = select_images(mask_rows, image_owner)
        key_rows = image_keys[slot_ids]
        value_rows = image_values[slot_ids]
        query_grad, key_grad, value_grad, gate_part = group_backward(query_rows, cot_rows, key_rows, value_rows, keep_mask, gate_value)
        stacked = jnp.concatenate([key_grad.reshape(RMAX, IMG_TOK, KVH * HD), value_grad.reshape(RMAX, IMG_TOK, KVH * HD)], axis=-1)
        stacked = jnp.where(is_read[:, None, None], stacked, 0.0)
        grads_acc = grads_acc.at[slot_ids].add(stacked)
        return ((grads_acc, gate_acc + gate_part), query_grad)
    init_state = (jnp.zeros((NIMG, IMG_TOK, 2 * KVH * HD), jnp.float32), jnp.zeros((), jnp.float32))
    (grads_acc, gate_acc), query_all = lax.scan(group_step, init_state, (query_groups, cot_groups, mask_groups))
    key_grad = grads_acc[:, :, :KVH * HD].astype(jnp.bfloat16)
    value_grad = grads_acc[:, :, KVH * HD:].astype(jnp.bfloat16)
    gate_grad = ((1.0 - gate_value * gate_value) * gate_acc / math.sqrt(TEXT * H * HD)).reshape(1).astype(jnp.float32)
    return (query_all.reshape(TEXT, H * HD), key_grad, value_grad, gate_grad)
```

```python
import functools
import math

import jax
import jax.numpy as jnp
from jax import lax
from jax.experimental import pallas as pl
from jax.experimental.pallas import tpu as pltpu
from jax.sharding import PartitionSpec as P

HD = 128
HEADS = 8
TOK = 256
BLK = 128
IMG = 64
SLOTS = 64
READ = 32
KEYS = READ * IMG
CHUNK = 512
RA, RB = 16, 48
X, Y, Z = 4, 2, 8
TERMS = 16384 * 8192
SCALE = math.log2(math.e) / math.sqrt(HD)
NT = (((1,), (1,)), ((), ()))
F32 = jnp.float32
BF16 = jnp.bfloat16
MESH = pl.DeviceIdType.MESH
PLANE = [(dx, dy) for dy in range(Y) for dx in range(X) if dx + dy]
VM = pl.BlockSpec(memory_space=pltpu.VMEM)
SM = pl.BlockSpec(memory_space=pltpu.SMEM)


class Place:
    def __init__(self):
        ctx = lax.axis_index("ctx")
        self.tp = lax.axis_index("tp")
        self.x = lax.rem(ctx, X)
        self.z = lax.rem(ctx // X, Z)
        self.y = ctx // (X * Z)
        self.p = self.y * X + self.x

    def z_at(self, d):
        return lax.rem(self.z + d + Z, Z)

    def p_at(self, dx, dy):
        return lax.rem(self.y + dy, Y) * X + lax.rem(self.x + dx + X, X)

    def z_dev(self, d):
        return ((self.y * Z + self.z_at(d)) * X + self.x, self.tp)

    def p_dev(self, dx, dy):
        y, x = lax.rem(self.y + dy, Y), lax.rem(self.x + dx + X, X)
        return ((y * Z + self.z) * X + x, self.tp)

    def tp_dev(self, d):
        return ((self.y * Z + self.z) * X + self.x, lax.rem(self.tp + d, 8))


def greet(devices):
    barrier = pltpu.get_barrier_semaphore()
    for dev in devices:
        pl.semaphore_signal(barrier, inc=1, device_id=dev, device_id_type=MESH)
    pl.semaphore_wait(barrier, len(devices))


class Wires:
    def __init__(self, send_sem, recv_sem):
        self.send_sem, self.recv_sem, self.sent = send_sem, recv_sem, []

    def copy(self, src, dst, dev, i):
        return pltpu.make_async_remote_copy(
            src_ref=src,
            dst_ref=dst,
            send_sem=self.send_sem.at[i],
            recv_sem=self.recv_sem.at[i],
            device_id=dev,
            device_id_type=MESH,
        )

    def send(self, src, dst, dev, i):
        one = self.copy(src, dst, dev, i)
        one.start()
        self.sent.append(one)

    def arrived(self, dst, dev, i):
        self.copy(dst, dst, dev, i).wait_recv()

    def drain(self):
        for one in self.sent:
            one.wait_send()


def gather_first(me, wires, src, ga, gb, base):
    ga[me.z * 8 + me.p] = src[0, 0:RA]
    gb[me.p * 8 + me.z] = src[0, RA:IMG]
    for d in range(1, Z):
        spot = gb.at[me.p * 8 + me.z]
        wires.send(spot, spot, me.z_dev(d), base + d)
    for i, (dx, dy) in enumerate(PLANE):
        spot = ga.at[me.z * 8 + me.p]
        wires.send(spot, spot, me.p_dev(dx, dy), base + 8 + i)


def gather_second(me, wires, ga, gb, base):
    for d in range(1, Z):
        wires.arrived(gb.at[me.p * 8 + me.z_at(-d)], me.z_dev(d), base + d)
    row = gb.at[pl.ds(me.p * 8, 8)]
    for i, (dx, dy) in enumerate(PLANE):
        wires.send(row, row, me.p_dev(dx, dy), base + 16 + i)
    for i, (dx, dy) in enumerate(PLANE):
        wires.arrived(ga.at[me.z * 8 + me.p_at(-dx, dy)], me.p_dev(dx, dy), base + 8 + i)
    row = ga.at[pl.ds(me.z * 8, 8)]
    for d in range(1, Z):
        wires.send(row, row, me.z_dev(d), base + 24 + d)


def gather_last(me, wires, ga, gb, base):
    for i, (dx, dy) in enumerate(PLANE):
        wires.arrived(gb.at[pl.ds(me.p_at(-dx, dy) * 8, 8)], me.p_dev(dx, dy), base + 16 + i)
    for d in range(1, Z):
        wires.arrived(ga.at[pl.ds(me.z_at(-d) * 8, 8)], me.z_dev(d), base + 24 + d)


def gather_kernel(k_ref, v_ref, ka, kb, va, vb, send_sem, recv_sem):
    me = Place()
    greet([me.z_dev(d) for d in range(1, Z)] + [me.p_dev(*d) for d in PLANE])
    wires = Wires(send_sem, recv_sem)
    gather_first(me, wires, k_ref, ka, kb, 0)
    gather_first(me, wires, v_ref, va, vb, 32)
    gather_second(me, wires, ka, kb, 0)
    gather_second(me, wires, va, vb, 32)
    gather_last(me, wires, ka, kb, 0)
    gather_last(me, wires, va, vb, 32)
    wires.drain()


def head_lanes(h):
    return pl.ds(pl.multiple_of(h * HD, HD), HD)


def find_reads(mask_ref, owner_ref, ids, pos):
    def image(i, n):
        slot, m0, m1 = owner_ref[i], mask_ref[0, i], mask_ref[1, i]
        read = ((m0 + m1) > 0).astype(jnp.int32)
        z, p = (slot // X) % Z, (slot // (X * Z)) * X + slot % X
        ids[0, n] = z * 8 + p
        ids[1, n] = p * 8 + z
        ids[2, n] = m0
        ids[3, n] = m1
        place = jnp.where(read > 0, n, READ)
        pos[0, z * 8 + p] = place
        pos[1, p * 8 + z] = place
        return n + read

    lax.fori_loop(0, SLOTS, image, 0)


def pick_rows(ids, a_ref, b_ref, dst, with_bias):
    lane = lax.broadcasted_iota(jnp.int32, (IMG, HD), 1)
    for j in range(READ):
        at = j * IMG
        dst[at : at + RA, 0:HD] = a_ref[ids[0, j]]
        dst[at + RA : at + IMG, 0:HD] = b_ref[ids[1, j]]
        if with_bias:
            b0 = jnp.where(ids[2, j] > 0, 0.0, -1e30)
            b1 = jnp.where(ids[3, j] > 0, 0.0, -1e30)
            bias = jnp.where(lane == 0, b0, jnp.where(lane == 1, b1, 0.0))
            dst[at : at + IMG, HD : 2 * HD] = bias.astype(BF16)


def softmax_and_values(q_ref, c_ref, kc, s_ref, p_ref, dv_ref):
    lane = lax.broadcasted_iota(jnp.int32, (TOK, HD), 1)
    row = lax.broadcasted_iota(jnp.int32, (TOK, HD), 0)
    block_of = (lane == row // BLK).astype(BF16)
    dv_ref[...] = jnp.zeros_like(dv_ref)

    def head(h, _):
        query = jnp.concatenate([q_ref[:, head_lanes(h)], block_of], axis=1)
        top = jnp.full((8, TOK), -jnp.inf, F32)
        for k in range(0, KEYS, CHUNK):
            s = lax.dot_general(kc[k : k + CHUNK, :], query, NT, preferred_element_type=F32)
            s_ref[k : k + CHUNK, :] = s
            top = jnp.maximum(top, jnp.max(s.reshape(CHUNK // 8, 8, TOK), axis=0))
        top = jnp.max(top, axis=0, keepdims=True) * SCALE
        total = jnp.zeros((8, TOK), F32)
        for k in range(0, KEYS, CHUNK):
            e = jnp.exp2(s_ref[k : k + CHUNK, :] * SCALE - top)
            total = total + jnp.sum(e.reshape(CHUNK // 8, 8, TOK), axis=0)
            s_ref[k : k + CHUNK, :] = e
        inverse = 1.0 / jnp.sum(total, axis=0, keepdims=True)
        cot = c_ref[:, head_lanes(h)]
        for k in range(0, KEYS, CHUNK):
            prob = (s_ref[k : k + CHUNK, :] * inverse).astype(BF16)
            p_ref[h, k : k + CHUNK, :] = prob
            dv_ref[k : k + CHUNK, :] += jnp.dot(prob, cot, preferred_element_type=F32)
        return 0

    lax.fori_loop(0, HEADS, head, 0)


def score_and_keys(q_ref, c_ref, vc, s_ref, p_ref, ds_ref, dk_ref, gate_ref):
    dk_ref[...] = jnp.zeros_like(dk_ref)
    gate_ref[...] = jnp.zeros_like(gate_ref)

    def head(h, _):
        cot = c_ref[:, head_lanes(h)]
        delta = jnp.zeros((8, TOK), F32)
        for k in range(0, KEYS, CHUNK):
            dp = lax.dot_general(vc[k : k + CHUNK, :], cot, NT, preferred_element_type=F32)
            s_ref[k : k + CHUNK, :] = dp
            part = dp * p_ref[h, k : k + CHUNK, :].astype(F32)
            delta = delta + jnp.sum(part.reshape(CHUNK // 8, 8, TOK), axis=0)
        gate_ref[...] += delta
        delta = jnp.sum(delta, axis=0, keepdims=True)
        query = q_ref[:, head_lanes(h)]
        for k in range(0, KEYS, CHUNK):
            prob = p_ref[h, k : k + CHUNK, :].astype(F32)
            ds = (prob * (s_ref[k : k + CHUNK, :] - delta)).astype(BF16)
            ds_ref[h, k : k + CHUNK, :] = ds
            dk_ref[k : k + CHUNK, :] += jnp.dot(ds, query, preferred_element_type=F32)
        return 0

    lax.fori_loop(0, HEADS, head, 0)


def queries_grad(kt, ds_ref, dq_ref, scale):
    def head(h, _):
        t = jnp.dot(kt[...], ds_ref[h], preferred_element_type=F32) * scale
        dq_ref[:, head_lanes(h)] = t.T.astype(BF16)
        return 0

    lax.fori_loop(0, HEADS, head, 0)


def spread_rows(pos, acc, a_ref, b_ref, scale):
    for s in range(SLOTS):
        a_ref[s] = (acc[pl.ds(pl.multiple_of(pos[0, s] * IMG, IMG), RA), :] * scale).astype(BF16)
        at = pl.multiple_of(pos[1, s] * IMG + RA, 16)
        b_ref[s] = (acc[pl.ds(at, RB), :] * scale).astype(BF16)


def local_kernel(
    mask_ref, owner_ref, gate_in, q_ref, c_ref, ka, kb, va, vb,
    dq_ref, dka, dkb, dva, dvb, gate_ref,
    ids, pos, kc, vc, kt, s_ref, p_ref, ds_ref, dk_ref, dv_ref,
):
    gate = jnp.tanh(jnp.full((1, HD), gate_in[0], F32))
    find_reads(mask_ref, owner_ref, ids, pos)
    pick_rows(ids, ka, kb, kc, True)
    pick_rows(ids, va, vb, vc, False)
    kt[...] = kc[:, 0:HD].T
    dk_ref[KEYS:, :] = jnp.zeros((IMG, HD), F32)
    dv_ref[KEYS:, :] = jnp.zeros((IMG, HD), F32)
    softmax_and_values(q_ref, c_ref, kc, s_ref, p_ref, dv_ref)
    spread_rows(pos, dv_ref, dva, dvb, gate)
    score_and_keys(q_ref, c_ref, vc, s_ref, p_ref, ds_ref, dk_ref, gate_ref)
    scale = gate * (1.0 / math.sqrt(HD))
    spread_rows(pos, dk_ref, dka, dkb, scale)
    queries_grad(kt, ds_ref, dq_ref, jnp.concatenate([scale, scale], axis=1))


def reduce_first(me, wires, sa, sb, ra, rb, base):
    for i, (dx, dy) in enumerate(PLANE):
        there = pl.ds(me.p_at(dx, dy) * 8, 8)
        wires.send(sb.at[there], rb.at[pl.ds(me.p * 8, 8)], me.p_dev(dx, dy), base + i)
    for d in range(1, Z):
        there = pl.ds(me.z_at(d) * 8, 8)
        wires.send(sa.at[there], ra.at[pl.ds(me.z * 8, 8)], me.z_dev(d), base + 8 + d)


def reduce_second(me, wires, sa, sb, ra, rb, ta, tb, ua, ub, base):
    total = sb[pl.ds(me.p * 8, 8)].astype(F32)
    for i, (dx, dy) in enumerate(PLANE):
        rows = pl.ds(me.p_at(-dx, dy) * 8, 8)
        wires.arrived(rb.at[rows], me.p_dev(dx, dy), base + i)
        total = total + rb[rows].astype(F32)
    tb[...] = total.astype(BF16)
    for d in range(1, Z):
        wires.send(tb.at[me.z_at(d)], ub.at[me.z], me.z_dev(d), base + 16 + d)
    total = sa[pl.ds(me.z * 8, 8)].astype(F32)
    for d in range(1, Z):
        rows = pl.ds(me.z_at(-d) * 8, 8)
        wires.arrived(ra.at[rows], me.z_dev(d), base + 8 + d)
        total = total + ra[rows].astype(F32)
    ta[...] = total.astype(BF16)
    for i, (dx, dy) in enumerate(PLANE):
        wires.send(ta.at[me.p_at(dx, dy)], ua.at[me.p], me.p_dev(dx, dy), base + 24 + i)


def reduce_last(me, wires, ta, tb, ua, ub, out, base):
    total = tb[me.z].astype(F32)
    for d in range(1, Z):
        wires.arrived(ub.at[me.z_at(-d)], me.z_dev(d), base + 16 + d)
        total = total + ub[me.z_at(-d)].astype(F32)
    out[0, RA:IMG] = total.astype(BF16)
    total = ta[me.p].astype(F32)
    for i, (dx, dy) in enumerate(PLANE):
        wires.arrived(ua.at[me.p_at(-dx, dy)], me.p_dev(dx, dy), base + 24 + i)
        total = total + ua[me.p_at(-dx, dy)].astype(F32)
    out[0, 0:RA] = total.astype(BF16)


def gate_step(wires, own, box, devices, places, base):
    for i, dev in enumerate(devices):
        wires.send(own, box.at[i], dev, base + i)

    def finish():
        total = own[...]
        for i, dev in enumerate(devices):
            wires.arrived(box.at[i], dev, base + i)
            total = total + box[i]
        return total

    return finish


def reduce_kernel(
    gate_in, dka, dkb, dva, dvb, gate_part, dk_out, dv_out, gate_out,
    rka, rkb, rva, rvb, tka, tkb, tva, tvb, uka, ukb, uva, uvb, gate_own, gate_box, send_sem, recv_sem,
):
    me = Place()
    along_z = [me.z_dev(d) for d in range(1, Z)]
    in_plane = [me.p_dev(*d) for d in PLANE]
    along_tp = [me.tp_dev(d) for d in range(1, 8)]
    greet(along_z + in_plane + along_tp)
    wires = Wires(send_sem, recv_sem)
    gate_own[0] = gate_part[:, 0:HD] + gate_part[:, HD : 2 * HD]
    step = gate_step(wires, gate_own.at[0], gate_box.at[0], along_z, None, 64)
    reduce_first(me, wires, dva, dvb, rva, rvb, 0)
    reduce_first(me, wires, dka, dkb, rka, rkb, 32)
    gate_own[1] = step()
    step = gate_step(wires, gate_own.at[1], gate_box.at[1], in_plane, None, 71)
    reduce_second(me, wires, dva, dvb, rva, rvb, tva, tvb, uva, uvb, 0)
    gate_own[2] = step()
    step = gate_step(wires, gate_own.at[2], gate_box.at[2], along_tp, None, 78)
    reduce_second(me, wires, dka, dkb, rka, rkb, tka, tkb, uka, ukb, 32)
    reduce_last(me, wires, tva, tvb, uva, uvb, dv_out, 0)
    reduce_last(me, wires, tka, tkb, uka, ukb, dk_out, 32)
    gate = jnp.tanh(jnp.full((8, HD), gate_in[0], F32))
    gate_out[0] = jnp.sum((1.0 - gate * gate) * step()) * (1.0 / math.sqrt(TERMS))
    wires.drain()


def per_device(queries, cotangent, image_keys, image_values, attn_gate, block_mask, image_owner):
    shape = jax.ShapeDtypeStruct
    rows_a, rows_b = shape((SLOTS, RA, HD), BF16), shape((SLOTS, RB, HD), BF16)
    dma = pltpu.SemaphoreType.DMA
    gathered = pl.pallas_call(
        gather_kernel,
        out_shape=[rows_a, rows_b, rows_a, rows_b],
        in_specs=[VM] * 2,
        out_specs=[VM] * 4,
        scratch_shapes=[dma((64,))] * 2,
        compiler_params=pltpu.CompilerParams(
            collective_id=0, has_side_effects=True, vmem_limit_bytes=16 << 20
        ),
    )(image_keys, image_values)
    dq, dka, dkb, dva, dvb, gate_part = pl.pallas_call(
        local_kernel,
        out_shape=[shape((TOK, HEADS * HD), BF16), rows_a, rows_b, rows_a, rows_b, shape((8, TOK), F32)],
        in_specs=[SM] * 3 + [VM] * 6,
        out_specs=[VM] * 6,
        scratch_shapes=[
            pltpu.SMEM((4, READ + 1), jnp.int32),
            pltpu.SMEM((2, SLOTS), jnp.int32),
            pltpu.VMEM((KEYS, 2 * HD), BF16),
            pltpu.VMEM((KEYS, HD), BF16),
            pltpu.VMEM((HD, KEYS), BF16),
            pltpu.VMEM((KEYS, TOK), F32),
            pltpu.VMEM((HEADS, KEYS, TOK), BF16),
            pltpu.VMEM((HEADS, KEYS, TOK), BF16),
            pltpu.VMEM((KEYS + IMG, HD), F32),
            pltpu.VMEM((KEYS + IMG, HD), F32),
        ],
        compiler_params=pltpu.CompilerParams(vmem_limit_bytes=48 << 20),
    )(block_mask, image_owner, attn_gate, queries, cotangent, *gathered)
    part_a, part_b = pltpu.VMEM((8, RA, HD), BF16), pltpu.VMEM((8, RB, HD), BF16)
    whole_a, whole_b = pltpu.VMEM((SLOTS, RA, HD), BF16), pltpu.VMEM((SLOTS, RB, HD), BF16)
    grad = shape((1, IMG, HD), BF16)
    dk, dv, gate = pl.pallas_call(
        reduce_kernel,
        out_shape=[grad, grad, shape((1,), F32)],
        in_specs=[SM] + [VM] * 5,
        out_specs=[VM, VM, SM],
        scratch_shapes=[whole_a, whole_b] * 2
        + [part_a, part_b] * 4
        + [pltpu.VMEM((3, 8, HD), F32), pltpu.VMEM((3, 7, 8, HD), F32), dma((88,)), dma((88,))],
        compiler_params=pltpu.CompilerParams(
            collective_id=1, has_side_effects=True, vmem_limit_bytes=24 << 20
        ),
    )(attn_gate, dka, dkb, dva, dvb, gate_part)
    return dq, dk, dv, gate


def solution(mesh):
    specs = (P("ctx", "tp"), P("ctx", "tp"), P("ctx", None, "tp"), P("ctx", None, "tp"), P(), P("ctx", None), P())
    outs = (P("ctx", "tp"), P("ctx", None, "tp"), P("ctx", None, "tp"), P())
    return jax.shard_map(per_device, mesh=mesh, in_specs=specs, out_specs=outs, check_vma=False)
```

```python
import functools
import math

import jax
import jax.numpy as jnp
from jax import lax
from jax.experimental import pallas as pl
from jax.experimental.pallas import tpu as pltpu
from jax.sharding import PartitionSpec as P

HD = 128
HEADS = 8
TOK = 256
BLK = 128
IMG = 64
SLOTS = 64
READ = 32
KEYS = READ * IMG
CHUNK = 512
RA, RB = 16, 48
X, Y, Z = 4, 2, 8
TERMS = 16384 * 8192
SCALE = math.log2(math.e) / math.sqrt(HD)
NT = (((1,), (1,)), ((), ()))
F32 = jnp.float32
BF16 = jnp.bfloat16
MESH = pl.DeviceIdType.MESH
PLANE = [(dx, dy) for dy in range(Y) for dx in range(X) if dx + dy]
VM = pl.BlockSpec(memory_space=pltpu.VMEM)
SM = pl.BlockSpec(memory_space=pltpu.SMEM)


class Place:
    def __init__(self):
        ctx = lax.axis_index("ctx")
        self.tp = lax.axis_index("tp")
        self.x = lax.rem(ctx, X)
        self.z = lax.rem(ctx // X, Z)
        self.y = ctx // (X * Z)
        self.p = self.y * X + self.x

    def z_at(self, d):
        return lax.rem(self.z + d + Z, Z)

    def p_at(self, dx, dy):
        return lax.rem(self.y + dy, Y) * X + lax.rem(self.x + dx + X, X)

    def z_dev(self, d):
        return ((self.y * Z + self.z_at(d)) * X + self.x, self.tp)

    def p_dev(self, dx, dy):
        y, x = lax.rem(self.y + dy, Y), lax.rem(self.x + dx + X, X)
        return ((y * Z + self.z) * X + x, self.tp)

    def tp_dev(self, d):
        return ((self.y * Z + self.z) * X + self.x, lax.rem(self.tp + d, 8))


def greet(devices):
    barrier = pltpu.get_barrier_semaphore()
    for dev in devices:
        pl.semaphore_signal(barrier, inc=1, device_id=dev, device_id_type=MESH)
    pl.semaphore_wait(barrier, len(devices))


class Wires:
    def __init__(self, send_sem, recv_sem):
        self.send_sem, self.recv_sem, self.sent = send_sem, recv_sem, []

    def copy(self, src, dst, dev, i):
        return pltpu.make_async_remote_copy(
            src_ref=src,
            dst_ref=dst,
            send_sem=self.send_sem.at[i],
            recv_sem=self.recv_sem.at[i],
            device_id=dev,
            device_id_type=MESH,
        )

    def send(self, src, dst, dev, i):
        one = self.copy(src, dst, dev, i)
        one.start()
        self.sent.append(one)

    def arrived(self, dst, dev, i):
        self.copy(dst, dst, dev, i).wait_recv()

    def drain(self):
        for one in self.sent:
            one.wait_send()


def gather_first(me, wires, src, ga, gb, base):
    for d in range(1, Z):
        wires.send(src.at[0, RA:IMG], gb.at[me.p * 8 + me.z], me.z_dev(d), base + d)
    for i, (dx, dy) in enumerate(PLANE):
        wires.send(src.at[0, 0:RA], ga.at[me.z * 8 + me.p], me.p_dev(dx, dy), base + 8 + i)


def gather_second(me, wires, ga, gb, base):
    for d in range(1, Z):
        wires.arrived(gb.at[me.p * 8 + me.z_at(-d)], me.z_dev(d), base + d)
    row = gb.at[pl.ds(me.p * 8, 8)]
    for i, (dx, dy) in enumerate(PLANE):
        wires.send(row, row, me.p_dev(dx, dy), base + 16 + i)
    for i, (dx, dy) in enumerate(PLANE):
        wires.arrived(ga.at[me.z * 8 + me.p_at(-dx, dy)], me.p_dev(dx, dy), base + 8 + i)
    row = ga.at[pl.ds(me.z * 8, 8)]
    for d in range(1, Z):
        wires.send(row, row, me.z_dev(d), base + 24 + d)


def gather_last(me, wires, ga, gb, base):
    for i, (dx, dy) in enumerate(PLANE):
        wires.arrived(gb.at[pl.ds(me.p_at(-dx, dy) * 8, 8)], me.p_dev(dx, dy), base + 16 + i)
    for d in range(1, Z):
        wires.arrived(ga.at[pl.ds(me.z_at(-d) * 8, 8)], me.z_dev(d), base + 24 + d)


def head_lanes(h):
    return pl.ds(pl.multiple_of(h * HD, HD), HD)


def find_reads(mask_ref, owner_ref, table):
    down = lax.broadcasted_iota(jnp.int32, (SLOTS, HD), 0)
    across = lax.broadcasted_iota(jnp.int32, (SLOTS, HD), 1)

    def image(i, reads):
        slot = owner_ref[i]
        hit = down == ((slot // X) % Z) * 8 + (slot // (X * Z)) * X + slot % X
        return tuple(jnp.where(hit, mask_ref[b, i], r) for b, r in enumerate(reads))

    def total(where, what):
        return jnp.sum(jnp.where(where, what, 0), axis=0, keepdims=True)

    zero = jnp.zeros((SLOTS, HD), jnp.int32)
    first, second = lax.fori_loop(0, SLOTS, image, (zero, zero))
    read = jnp.minimum(first + second, 1)
    position = jnp.where(total(down == across, read) > 0, total(down < across, read), READ)
    chosen = jnp.broadcast_to(position, (HD, HD)).T[0:SLOTS] == across
    sub = lax.broadcasted_iota(jnp.int32, (8, HD), 0)
    low = jnp.where(sub == 0, total(chosen, down), total(chosen, first))
    high = jnp.where(sub == 2, total(chosen, second), position)
    turned = lax.rem(down, 8) * 8 + down // 8
    table[...] = jnp.where(sub < 2, low, jnp.where(sub < 4, high, total(chosen, turned)))


def pick_rows(table, a_ref, b_ref, dst, with_bias):
    lane = lax.broadcasted_iota(jnp.int32, (IMG, HD), 1)
    for j in range(READ):
        at = j * IMG
        place = table[0, j]
        dst[at : at + RA, 0:HD] = a_ref[place]
        dst[at + RA : at + IMG, 0:HD] = b_ref[table[4, j]]
        if with_bias:
            b0 = jnp.where(table[1, j] > 0, 0.0, -1e30)
            b1 = jnp.where(table[2, j] > 0, 0.0, -1e30)
            bias = jnp.where(lane == 0, b0, jnp.where(lane == 1, b1, 0.0))
            dst[at : at + IMG, HD : 2 * HD] = bias.astype(BF16)


def softmax_and_values(q_ref, c_ref, kc, s_ref, p_ref, dv_ref):
    lane = lax.broadcasted_iota(jnp.int32, (TOK, HD), 1)
    row = lax.broadcasted_iota(jnp.int32, (TOK, HD), 0)
    block_of = (lane == row // BLK).astype(BF16)
    dv_ref[...] = jnp.zeros_like(dv_ref)

    def head(h, _):
        query = jnp.concatenate([q_ref[:, head_lanes(h)], block_of], axis=1)
        top = jnp.full((8, TOK), -jnp.inf, F32)
        for k in range(0, KEYS, CHUNK):
            s = lax.dot_general(kc[k : k + CHUNK, :], query, NT, preferred_element_type=F32)
            s_ref[k : k + CHUNK, :] = s
            top = jnp.maximum(top, jnp.max(s.reshape(CHUNK // 8, 8, TOK), axis=0))
        top = jnp.max(top, axis=0, keepdims=True) * SCALE
        total = jnp.zeros((8, TOK), F32)
        for k in range(0, KEYS, CHUNK):
            e = jnp.exp2(s_ref[k : k + CHUNK, :] * SCALE - top)
            total = total + jnp.sum(e.reshape(CHUNK // 8, 8, TOK), axis=0)
            s_ref[k : k + CHUNK, :] = e
        inverse = 1.0 / jnp.sum(total, axis=0, keepdims=True)
        cot = c_ref[:, head_lanes(h)]
        for k in range(0, KEYS, CHUNK):
            prob = (s_ref[k : k + CHUNK, :] * inverse).astype(BF16)
            p_ref[h, k : k + CHUNK, :] = prob
            part = jnp.dot(prob, cot, preferred_element_type=F32)
            dv_ref[k // IMG : (k + CHUNK) // IMG] += part.reshape(CHUNK // IMG, IMG, HD)
        return 0

    lax.fori_loop(0, HEADS, head, 0)


def score_and_keys(q_ref, c_ref, vc, s_ref, p_ref, ds_ref, dk_ref, gate_ref):
    dk_ref[...] = jnp.zeros_like(dk_ref)
    gate_ref[...] = jnp.zeros_like(gate_ref)

    def head(h, _):
        cot = c_ref[:, head_lanes(h)]
        delta = jnp.zeros((8, TOK), F32)
        for k in range(0, KEYS, CHUNK):
            dp = lax.dot_general(vc[k : k + CHUNK, :], cot, NT, preferred_element_type=F32)
            s_ref[k : k + CHUNK, :] = dp
            part = dp * p_ref[h, k : k + CHUNK, :].astype(F32)
            delta = delta + jnp.sum(part.reshape(CHUNK // 8, 8, TOK), axis=0)
        gate_ref[...] += delta
        delta = jnp.sum(delta, axis=0, keepdims=True)
        query = q_ref[:, head_lanes(h)]
        for k in range(0, KEYS, CHUNK):
            prob = p_ref[h, k : k + CHUNK, :].astype(F32)
            ds = (prob * (s_ref[k : k + CHUNK, :] - delta)).astype(BF16)
            ds_ref[h, k : k + CHUNK, :] = ds
            part = jnp.dot(ds, query, preferred_element_type=F32)
            dk_ref[k // IMG : (k + CHUNK) // IMG] += part.reshape(CHUNK // IMG, IMG, HD)
        return 0

    lax.fori_loop(0, HEADS, head, 0)


def queries_grad(kt, ds_ref, dq_ref, scale):
    def head(h, _):
        t = jnp.dot(kt[...], ds_ref[h], preferred_element_type=F32) * scale
        dq_ref[:, head_lanes(h)] = t.T.astype(BF16)
        return 0

    lax.fori_loop(0, HEADS, head, 0)


def spread_rows(table, acc, a_ref, b_ref, scale):
    for s in range(SLOTS):
        a_ref[s] = (acc[table[3, s], 0:RA] * scale).astype(BF16)
        b_ref[s] = (acc[table[3, (s % 8) * 8 + s // 8], RA:IMG] * scale).astype(BF16)


def reduce_first(me, wires, sa, sb, ra, rb, base):
    for i, (dx, dy) in enumerate(PLANE):
        there = pl.ds(me.p_at(dx, dy) * 8, 8)
        wires.send(sb.at[there], rb.at[pl.ds(me.p * 8, 8)], me.p_dev(dx, dy), base + i)
    for d in range(1, Z):
        there = pl.ds(me.z_at(d) * 8, 8)
        wires.send(sa.at[there], ra.at[pl.ds(me.z * 8, 8)], me.z_dev(d), base + 8 + d)


def reduce_second(me, wires, sa, sb, ra, rb, ta, tb, ua, ub, base):
    total = sb[pl.ds(me.p * 8, 8)].astype(F32)
    for i, (dx, dy) in enumerate(PLANE):
        rows = pl.ds(me.p_at(-dx, dy) * 8, 8)
        wires.arrived(rb.at[rows], me.p_dev(dx, dy), base + i)
        total = total + rb[rows].astype(F32)
    tb[...] = total.astype(BF16)
    for d in range(1, Z):
        wires.send(tb.at[me.z_at(d)], ub.at[me.z], me.z_dev(d), base + 16 + d)
    total = sa[pl.ds(me.z * 8, 8)].astype(F32)
    for d in range(1, Z):
        rows = pl.ds(me.z_at(-d) * 8, 8)
        wires.arrived(ra.at[rows], me.z_dev(d), base + 8 + d)
        total = total + ra[rows].astype(F32)
    ta[...] = total.astype(BF16)
    for i, (dx, dy) in enumerate(PLANE):
        wires.send(ta.at[me.p_at(dx, dy)], ua.at[me.p], me.p_dev(dx, dy), base + 24 + i)


def reduce_last(me, wires, ta, tb, ua, ub, out, base):
    total = tb[me.z].astype(F32)
    for d in range(1, Z):
        wires.arrived(ub.at[me.z_at(-d)], me.z_dev(d), base + 16 + d)
        total = total + ub[me.z_at(-d)].astype(F32)
    out[0, RA:IMG] = total.astype(BF16)
    total = ta[me.p].astype(F32)
    for i, (dx, dy) in enumerate(PLANE):
        wires.arrived(ua.at[me.p_at(-dx, dy)], me.p_dev(dx, dy), base + 24 + i)
        total = total + ua[me.p_at(-dx, dy)].astype(F32)
    out[0, 0:RA] = total.astype(BF16)


def gate_step(wires, own, box, devices, base):
    for i, dev in enumerate(devices):
        wires.send(own, box.at[i], dev, base + i)

    def finish():
        total = own[...]
        for i, dev in enumerate(devices):
            wires.arrived(box.at[i], dev, base + i)
            total = total + box[i]
        return total

    return finish


def kernel(
    mask_in, owner_in, gate_in, q_in, c_in, k_in, v_in, dq_out, dk_out, dv_out, gate_out,
    mask_ref, owner_ref, gate_ref, table_v, table, q_ref, c_ref, dq_ref,
    ka, kb, va, vb, kc, vc, kt, s_ref, p_ref, ds_ref, dk_ref, dv_ref,
    dka, dkb, dva, dvb, rka, rkb, rva, rvb, tka, tkb, tva, tvb, uka, ukb, uva, uvb,
    gate_rows, gate_own, gate_box, local_sem, send_sem, recv_sem,
):
    me = Place()
    along_z = [me.z_dev(d) for d in range(1, Z)]
    in_plane = [me.p_dev(*d) for d in PLANE]
    along_tp = [me.tp_dev(d) for d in range(1, 8)]
    here_a, here_b = me.z * 8 + me.p, me.p * 8 + me.z
    inputs = [
        pltpu.make_async_copy(src, dst, local_sem.at[i])
        for i, (src, dst) in enumerate(
            (
                (k_in.at[0, 0:RA], ka.at[here_a]),
                (k_in.at[0, RA:IMG], kb.at[here_b]),
                (v_in.at[0, 0:RA], va.at[here_a]),
                (v_in.at[0, RA:IMG], vb.at[here_b]),
                (mask_in, mask_ref),
                (owner_in, owner_ref),
                (gate_in, gate_ref),
                (q_in, q_ref),
                (c_in, c_ref),
            )
        )
    ]
    for one in inputs:
        one.start()
    greet(along_z + in_plane + along_tp)
    wires = Wires(send_sem, recv_sem)
    gather_first(me, wires, k_in, ka, kb, 0)
    gather_first(me, wires, v_in, va, vb, 32)
    for one in inputs:
        one.wait()
    gate = jnp.tanh(jnp.full((1, HD), gate_ref[0], F32))
    find_reads(mask_ref, owner_ref, table_v)
    put = pltpu.make_async_copy(table_v, table, local_sem.at[9])
    put.start()
    dk_ref[READ] = jnp.zeros((IMG, HD), F32)
    dv_ref[READ] = jnp.zeros((IMG, HD), F32)
    put.wait()
    gather_second(me, wires, ka, kb, 0)
    gather_last(me, wires, ka, kb, 0)
    gather_second(me, wires, va, vb, 32)
    pick_rows(table, ka, kb, kc, True)
    kt[...] = kc[:, 0:HD].T
    softmax_and_values(q_ref, c_ref, kc, s_ref, p_ref, dv_ref)
    spread_rows(table, dv_ref, dva, dvb, gate)
    reduce_first(me, wires, dva, dvb, rva, rvb, 64)
    gather_last(me, wires, va, vb, 32)
    pick_rows(table, va, vb, vc, False)
    score_and_keys(q_ref, c_ref, vc, s_ref, p_ref, ds_ref, dk_ref, gate_rows)
    scale = gate * (1.0 / math.sqrt(HD))
    spread_rows(table, dk_ref, dka, dkb, scale)
    reduce_first(me, wires, dka, dkb, rka, rkb, 96)
    gate_own[0] = gate_rows[:, 0:HD] + gate_rows[:, HD : 2 * HD]
    step = gate_step(wires, gate_own.at[0], gate_box.at[0], along_z, 128)
    reduce_second(me, wires, dva, dvb, rva, rvb, tva, tvb, uva, uvb, 64)
    queries_grad(kt, ds_ref, dq_ref, jnp.concatenate([scale, scale], axis=1))
    back = pltpu.make_async_copy(dq_ref, dq_out, local_sem.at[10])
    back.start()
    gate_own[1] = step()
    step = gate_step(wires, gate_own.at[1], gate_box.at[1], in_plane, 135)
    reduce_last(me, wires, tva, tvb, uva, uvb, dv_out, 64)
    gate_own[2] = step()
    step = gate_step(wires, gate_own.at[2], gate_box.at[2], along_tp, 142)
    reduce_second(me, wires, dka, dkb, rka, rkb, tka, tkb, uka, ukb, 96)
    gate = jnp.tanh(jnp.full((8, HD), gate_ref[0], F32))
    gate_out[0] = jnp.sum((1.0 - gate * gate) * step()) * (1.0 / math.sqrt(TERMS))
    reduce_last(me, wires, tka, tkb, uka, ukb, dk_out, 96)
    back.wait()
    wires.drain()


def per_device(queries, cotangent, image_keys, image_values, attn_gate, block_mask, image_owner):
    shape = jax.ShapeDtypeStruct
    dma = pltpu.SemaphoreType.DMA
    rows = shape((TOK, HEADS * HD), BF16)
    rows_here = pltpu.VMEM((TOK, HEADS * HD), BF16)
    part_a, part_b = pltpu.VMEM((8, RA, HD), BF16), pltpu.VMEM((8, RB, HD), BF16)
    whole_a, whole_b = pltpu.VMEM((SLOTS, RA, HD), BF16), pltpu.VMEM((SLOTS, RB, HD), BF16)
    grad = shape((1, IMG, HD), BF16)
    anywhere = pl.BlockSpec(memory_space=pltpu.HBM)
    return pl.pallas_call(
        kernel,
        out_shape=[rows, grad, grad, shape((1,), F32)],
        in_specs=[anywhere] * 7,
        out_specs=[anywhere, VM, VM, SM],
        scratch_shapes=[
            pltpu.SMEM((2, SLOTS), jnp.int32),
            pltpu.SMEM((SLOTS,), jnp.int32),
            pltpu.SMEM((1,), F32),
            pltpu.VMEM((8, HD), jnp.int32),
            pltpu.SMEM((8, HD), jnp.int32),
            rows_here,
            rows_here,
            rows_here,
        ]
        + [whole_a, whole_b] * 2
        + [
            pltpu.VMEM((KEYS, 2 * HD), BF16),
            pltpu.VMEM((KEYS, HD), BF16),
            pltpu.VMEM((HD, KEYS), BF16),
            pltpu.VMEM((KEYS, TOK), F32),
            pltpu.VMEM((HEADS, KEYS, TOK), BF16),
            pltpu.VMEM((HEADS, KEYS, TOK), BF16),
            pltpu.VMEM((READ + 1, IMG, HD), F32),
            pltpu.VMEM((READ + 1, IMG, HD), F32),
        ]
        + [whole_a, whole_b] * 4
        + [part_a, part_b] * 4
        + [pltpu.VMEM((8, TOK), F32), pltpu.VMEM((3, 8, HD), F32), pltpu.VMEM((3, 7, 8, HD), F32)]
        + [dma((11,)), dma((150,)), dma((150,))],
        compiler_params=pltpu.CompilerParams(
            collective_id=0, has_side_effects=True, vmem_limit_bytes=(64 << 20) - (64 << 10)
        ),
    )(block_mask, image_owner, attn_gate, queries, cotangent, image_keys, image_values)


def solution(mesh):
    specs = (P("ctx", "tp"), P("ctx", "tp"), P("ctx", None, "tp"), P("ctx", None, "tp"), P(), P("ctx", None), P())
    outs = (P("ctx", "tp"), P("ctx", None, "tp"), P("ctx", None, "tp"), P())
    return jax.shard_map(per_device, mesh=mesh, in_specs=specs, out_specs=outs, check_vma=False)
```

```python
import functools
import math

import jax
import jax.numpy as jnp
from jax import lax
from jax.experimental import pallas as pl
from jax.experimental.pallas import tpu as pltpu
from jax.sharding import PartitionSpec as P

HD = 128
HEADS = 8
TOK = 256
BLK = 128
IMG = 64
SLOTS = 64
READ = 32
KEYS = READ * IMG
CHUNK = 512
TOGETHER = 4
RA, RB = 16, 48
X, Y, Z = 4, 2, 8
TERMS = 16384 * 8192
SCALE = math.log2(math.e) / math.sqrt(HD)
NT = (((1,), (1,)), ((), ()))
F32 = jnp.float32
BF16 = jnp.bfloat16
MESH = pl.DeviceIdType.MESH
PLANE = [(dx, dy) for dy in range(Y) for dx in range(X) if dx + dy]
VM = pl.BlockSpec(memory_space=pltpu.VMEM)
SM = pl.BlockSpec(memory_space=pltpu.SMEM)


class Place:
    def __init__(self):
        ctx = lax.axis_index("ctx")
        self.tp = lax.axis_index("tp")
        self.x = lax.rem(ctx, X)
        self.z = lax.rem(ctx // X, Z)
        self.y = ctx // (X * Z)
        self.p = self.y * X + self.x

    def z_at(self, d):
        return lax.rem(self.z + d + Z, Z)

    def p_at(self, dx, dy):
        return lax.rem(self.y + dy, Y) * X + lax.rem(self.x + dx + X, X)

    def z_dev(self, d):
        return ((self.y * Z + self.z_at(d)) * X + self.x, self.tp)

    def p_dev(self, dx, dy):
        y, x = lax.rem(self.y + dy, Y), lax.rem(self.x + dx + X, X)
        return ((y * Z + self.z) * X + x, self.tp)

    def tp_dev(self, d):
        return ((self.y * Z + self.z) * X + self.x, lax.rem(self.tp + d, 8))


def greet(devices):
    barrier = pltpu.get_barrier_semaphore()
    for dev in devices:
        pl.semaphore_signal(barrier, inc=1, device_id=dev, device_id_type=MESH)
    pl.semaphore_wait(barrier, len(devices))


class Wires:
    def __init__(self, send_sem, recv_sem):
        self.send_sem, self.recv_sem, self.groups, self.gone = send_sem, recv_sem, {}, []

    def copy(self, src, dst, dev, group):
        return pltpu.make_async_remote_copy(
            src_ref=src,
            dst_ref=dst,
            send_sem=self.send_sem.at[group],
            recv_sem=self.recv_sem.at[group],
            device_id=dev,
            device_id_type=MESH,
        )

    def send(self, src, dst, dev, group):
        self.copy(src, dst, dev, group).start()

    def arrived(self, whole, dev, group):
        one = self.copy(whole, whole, dev, group)
        one.wait_recv()
        self.groups[group] = one

    def left(self, whole, dev, group):
        self.copy(whole, whole, dev, group).wait_send()
        self.gone.append(group)

    def drain(self):
        for group, one in self.groups.items():
            if group not in self.gone:
                one.wait_send()


def gather_first(me, wires, src, ga, gb, base):
    for d in range(1, Z):
        wires.send(src.at[0, RA:IMG], gb.at[me.p * 8 + me.z], me.z_dev(d), base)
    for dx, dy in PLANE:
        wires.send(src.at[0, 0:RA], ga.at[me.z * 8 + me.p], me.p_dev(dx, dy), base + 1)


def gather_second(me, wires, ga, gb, base):
    wires.arrived(gb.at[pl.ds(0, 7)], me.z_dev(1), base)
    row = gb.at[pl.ds(me.p * 8, 8)]
    for dx, dy in PLANE:
        wires.send(row, row, me.p_dev(dx, dy), base + 2)
    wires.arrived(ga.at[pl.ds(0, 7)], me.z_dev(1), base + 1)
    row = ga.at[pl.ds(me.z * 8, 8)]
    for d in range(1, Z):
        wires.send(row, row, me.z_dev(d), base + 3)


def gather_last(me, wires, ga, gb, base):
    wires.arrived(gb.at[pl.ds(0, 56)], me.z_dev(1), base + 2)
    wires.arrived(ga.at[pl.ds(0, 56)], me.z_dev(1), base + 3)


def head_lanes(h):
    return pl.ds(pl.multiple_of(h * HD, HD), HD)


def find_reads(mask_ref, owner_ref, table):
    down = lax.broadcasted_iota(jnp.int32, (SLOTS, HD), 0)
    across = lax.broadcasted_iota(jnp.int32, (SLOTS, HD), 1)

    def image(i, reads):
        slot = owner_ref[i]
        hit = down == ((slot // X) % Z) * 8 + (slot // (X * Z)) * X + slot % X
        return tuple(jnp.where(hit, mask_ref[b, i], r) for b, r in enumerate(reads))

    def total(where, what):
        return jnp.sum(jnp.where(where, what, 0), axis=0, keepdims=True)

    zero = jnp.zeros((SLOTS, HD), jnp.int32)
    first, second = lax.fori_loop(0, SLOTS, image, (zero, zero))
    read = jnp.minimum(first + second, 1)
    position = jnp.where(total(down == across, read) > 0, total(down < across, read), READ)
    chosen = jnp.broadcast_to(position, (HD, HD)).T[0:SLOTS] == across
    sub = lax.broadcasted_iota(jnp.int32, (8, HD), 0)
    low = jnp.where(sub == 0, total(chosen, down), total(chosen, first))
    high = jnp.where(sub == 2, total(chosen, second), position)
    turned = lax.rem(down, 8) * 8 + down // 8
    table[...] = jnp.where(sub < 2, low, jnp.where(sub < 4, high, total(chosen, turned)))


def mask_columns(table, dst):
    lane = lax.broadcasted_iota(jnp.int32, (IMG, HD), 1)
    for j in range(READ):
        b0 = jnp.where(table[1, j] > 0, 0.0, -1e30)
        b1 = jnp.where(table[2, j] > 0, 0.0, -1e30)
        bias = jnp.where(lane == 0, b0, jnp.where(lane == 1, b1, 0.0))
        dst[j * IMG : (j + 1) * IMG, HD : 2 * HD] = bias.astype(BF16)


def pick_rows(table, a_ref, b_ref, dst):
    for j in range(READ):
        at = j * IMG
        dst[at : at + RA, 0:HD] = a_ref[table[0, j]]
        dst[at + RA : at + IMG, 0:HD] = b_ref[table[4, j]]


def fold(x, op):
    return op(x.reshape(CHUNK // 8, 8, TOK), axis=0)


def add_rows(acc, k, part):
    acc[k // IMG : (k + CHUNK) // IMG] += part.reshape(CHUNK // IMG, IMG, HD)


def softmax_and_values(q_ref, c_ref, kc, s_ref, p_ref, dv_ref):
    lane = lax.broadcasted_iota(jnp.int32, (TOK, HD), 1)
    row = lax.broadcasted_iota(jnp.int32, (TOK, HD), 0)
    block_of = (lane == row // BLK).astype(BF16)
    chunks = range(0, KEYS, CHUNK)

    def some_heads(i, _):
        heads = [i * TOGETHER + j for j in range(TOGETHER)]
        query = [jnp.concatenate([q_ref[:, head_lanes(h)], block_of], axis=1) for h in heads]
        top = [jnp.full((8, TOK), -jnp.inf, F32) for _ in heads]
        for k in chunks:
            for j in range(TOGETHER):
                s = lax.dot_general(kc[k : k + CHUNK, :], query[j], NT, preferred_element_type=F32)
                top[j] = jnp.maximum(top[j], fold(s, jnp.max))
        top = [jnp.max(t, axis=0, keepdims=True) * SCALE for t in top]
        total = [jnp.zeros((8, TOK), F32) for _ in heads]
        for k in chunks:
            for j in range(TOGETHER):
                s = lax.dot_general(kc[k : k + CHUNK, :], query[j], NT, preferred_element_type=F32)
                e = jnp.exp2(s * SCALE - top[j])
                s_ref[j, k : k + CHUNK, :] = e
                total[j] = total[j] + fold(e, jnp.sum)
        inverse = [1.0 / jnp.sum(t, axis=0, keepdims=True) for t in total]
        cot = jnp.concatenate([c_ref[:, head_lanes(h)] for h in heads], axis=0)
        for k in chunks:
            probs = []
            for j, h in enumerate(heads):
                prob = (s_ref[j, k : k + CHUNK, :] * inverse[j]).astype(BF16)
                p_ref[h, k : k + CHUNK, :] = prob
                probs.append(prob)
            add_rows(dv_ref, k, jnp.dot(jnp.concatenate(probs, axis=1), cot, preferred_element_type=F32))
        return 0

    lax.fori_loop(0, HEADS // TOGETHER, some_heads, 0)


def score_and_keys(q_ref, c_ref, vc, s_ref, p_ref, ds_ref, dk_ref, gate_ref):
    chunks = range(0, KEYS, CHUNK)

    def some_heads(i, _):
        heads = [i * TOGETHER + j for j in range(TOGETHER)]
        cot = [c_ref[:, head_lanes(h)] for h in heads]
        delta = [jnp.zeros((8, TOK), F32) for _ in heads]
        for k in chunks:
            for j, h in enumerate(heads):
                dp = lax.dot_general(vc[k : k + CHUNK, :], cot[j], NT, preferred_element_type=F32)
                s_ref[j, k : k + CHUNK, :] = dp
                delta[j] = delta[j] + fold(dp * p_ref[h, k : k + CHUNK, :].astype(F32), jnp.sum)
        gate_ref[...] += sum(delta)
        delta = [jnp.sum(d, axis=0, keepdims=True) for d in delta]
        query = jnp.concatenate([q_ref[:, head_lanes(h)] for h in heads], axis=0)
        for k in chunks:
            grads = []
            for j, h in enumerate(heads):
                prob = p_ref[h, k : k + CHUNK, :].astype(F32)
                ds = (prob * (s_ref[j, k : k + CHUNK, :] - delta[j])).astype(BF16)
                ds_ref[h, k : k + CHUNK, :] = ds
                grads.append(ds)
            add_rows(dk_ref, k, jnp.dot(jnp.concatenate(grads, axis=1), query, preferred_element_type=F32))
        return 0

    lax.fori_loop(0, HEADS // TOGETHER, some_heads, 0)


def queries_grad(kt, ds_ref, dq_ref, scale):
    def head(h, _):
        t = jnp.dot(kt[...], ds_ref[h], preferred_element_type=F32) * scale
        dq_ref[:, head_lanes(h)] = t.T.astype(BF16)
        return 0

    lax.fori_loop(0, HEADS, head, 0)


def reduce_first(me, wires, table, acc, scale, sa, sb, ra, rb, base):
    def fill_b(p):
        for z in range(Z):
            sb[p * 8 + z] = (acc[table[3, z * 8 + p], RA:IMG] * scale).astype(BF16)

    def fill_a(z):
        for p in range(X * Y):
            sa[z * 8 + p] = (acc[table[3, z * 8 + p], 0:RA] * scale).astype(BF16)

    for dx, dy in PLANE:
        there = me.p_at(dx, dy)
        fill_b(there)
        wires.send(sb.at[pl.ds(there * 8, 8)], rb.at[pl.ds(me.p * 8, 8)], me.p_dev(dx, dy), base)
    for d in range(1, Z):
        there = me.z_at(d)
        fill_a(there)
        wires.send(sa.at[pl.ds(there * 8, 8)], ra.at[pl.ds(me.z * 8, 8)], me.z_dev(d), base + 1)
    fill_b(me.p)
    fill_a(me.z)


def reduce_second(me, wires, sa, sb, ra, rb, ta, tb, ua, ub, base):
    wires.arrived(rb.at[pl.ds(0, 56)], me.z_dev(1), base)
    total = sb[pl.ds(me.p * 8, 8)].astype(F32)
    for dx, dy in PLANE:
        total = total + rb[pl.ds(me.p_at(dx, dy) * 8, 8)].astype(F32)
    tb[...] = total.astype(BF16)
    for d in range(1, Z):
        wires.send(tb.at[me.z_at(d)], ub.at[me.z], me.z_dev(d), base + 2)
    wires.arrived(ra.at[pl.ds(0, 56)], me.z_dev(1), base + 1)
    total = sa[pl.ds(me.z * 8, 8)].astype(F32)
    for d in range(1, Z):
        total = total + ra[pl.ds(me.z_at(d) * 8, 8)].astype(F32)
    ta[...] = total.astype(BF16)
    for dx, dy in PLANE:
        wires.send(ta.at[me.p_at(dx, dy)], ua.at[me.p], me.p_dev(dx, dy), base + 3)


def reduce_last(me, wires, ta, tb, ua, ub, out, base):
    wires.arrived(ub.at[pl.ds(0, 7)], me.z_dev(1), base + 2)
    total = tb[me.z].astype(F32)
    for d in range(1, Z):
        total = total + ub[me.z_at(d)].astype(F32)
    out[0, RA:IMG] = total.astype(BF16)
    wires.arrived(ua.at[pl.ds(0, 7)], me.z_dev(1), base + 3)
    total = ta[me.p].astype(F32)
    for dx, dy in PLANE:
        total = total + ua[me.p_at(dx, dy)].astype(F32)
    out[0, 0:RA] = total.astype(BF16)


def gate_step(wires, own, box, devices, group):
    for i, dev in enumerate(devices):
        wires.send(own, box.at[i], dev, group)

    def finish():
        wires.arrived(box, devices[0], group)
        return own[...] + jnp.sum(box[...], axis=0)

    return finish


def kernel(
    mask_in, owner_in, gate_in, q_in, c_in, k_in, v_in, dq_out, dk_out, dv_out, gate_out,
    mask_ref, owner_ref, gate_ref, table_v, table, q_ref, c_ref, dq_ref,
    ka, kb, va, vb, kc, vc, kt, s_ref, p_ref, ds_ref, dk_ref, dv_ref,
    dka, dkb, dva, dvb, rka, rkb, rva, rvb, tka, tkb, tva, tvb, uka, ukb, uva, uvb,
    gate_rows, gate_own, gate_box, local_sem, send_sem, recv_sem,
):
    me = Place()
    along_z = [me.z_dev(d) for d in range(1, Z)]
    in_plane = [me.p_dev(*d) for d in PLANE]
    along_tp = [me.tp_dev(d) for d in range(1, 8)]
    here_a, here_b = me.z * 8 + me.p, me.p * 8 + me.z
    inputs = [
        pltpu.make_async_copy(src, dst, local_sem.at[i])
        for i, (src, dst) in enumerate(
            (
                (k_in.at[0, 0:RA], ka.at[here_a]),
                (k_in.at[0, RA:IMG], kb.at[here_b]),
                (v_in.at[0, 0:RA], va.at[here_a]),
                (v_in.at[0, RA:IMG], vb.at[here_b]),
                (mask_in, mask_ref),
                (owner_in, owner_ref),
                (gate_in, gate_ref),
                (q_in, q_ref),
                (c_in, c_ref),
            )
        )
    ]
    for one in inputs:
        one.start()
    greet(along_z + in_plane + along_tp)
    wires = Wires(send_sem, recv_sem)
    gather_first(me, wires, k_in, ka, kb, 0)
    gather_first(me, wires, v_in, va, vb, 4)
    for one in inputs:
        one.wait()
    gate = jnp.tanh(jnp.full((1, HD), gate_ref[0], F32))
    find_reads(mask_ref, owner_ref, table_v)
    put = pltpu.make_async_copy(table_v, table, local_sem.at[9])
    put.start()
    dk_ref[...] = jnp.zeros_like(dk_ref)
    dv_ref[...] = jnp.zeros_like(dv_ref)
    gate_rows[...] = jnp.zeros_like(gate_rows)
    put.wait()
    gather_second(me, wires, ka, kb, 0)
    mask_columns(table, kc)
    wires.left(kb.at[pl.ds(0, 56)], me.z_dev(1), 2)
    wires.left(ka.at[pl.ds(0, 56)], me.z_dev(1), 3)
    gather_second(me, wires, va, vb, 4)
    gather_last(me, wires, ka, kb, 0)
    pick_rows(table, ka, kb, kc)
    softmax_and_values(q_ref, c_ref, kc, s_ref, p_ref, dv_ref)
    reduce_first(me, wires, table, dv_ref, gate, dva, dvb, rva, rvb, 8)
    gather_last(me, wires, va, vb, 4)
    pick_rows(table, va, vb, vc)
    score_and_keys(q_ref, c_ref, vc, s_ref, p_ref, ds_ref, dk_ref, gate_rows)
    gate_own[0] = gate_rows[:, 0:HD] + gate_rows[:, HD : 2 * HD]
    step = gate_step(wires, gate_own.at[0], gate_box.at[0], along_z, 16)
    scale = gate * (1.0 / math.sqrt(HD))
    reduce_first(me, wires, table, dk_ref, scale, dka, dkb, rka, rkb, 12)
    kt[...] = kc[:, 0:HD].T
    queries_grad(kt, ds_ref, dq_ref, jnp.concatenate([scale, scale], axis=1))
    back = pltpu.make_async_copy(dq_ref, dq_out, local_sem.at[10])
    back.start()
    reduce_second(me, wires, dva, dvb, rva, rvb, tva, tvb, uva, uvb, 8)
    gate_own[1] = step()
    step = gate_step(wires, gate_own.at[1], gate_box.at[1], in_plane, 17)
    reduce_last(me, wires, tva, tvb, uva, uvb, dv_out, 8)
    gate_own[2] = step()
    step = gate_step(wires, gate_own.at[2], gate_box.at[2], along_tp, 18)
    reduce_second(me, wires, dka, dkb, rka, rkb, tka, tkb, uka, ukb, 12)
    reduce_last(me, wires, tka, tkb, uka, ukb, dk_out, 12)
    gate = jnp.tanh(jnp.full((8, HD), gate_ref[0], F32))
    gate_out[0] = jnp.sum((1.0 - gate * gate) * step()) * (1.0 / math.sqrt(TERMS))
    back.wait()
    wires.drain()


def hand_over(dq, dk, dv, gate, dq_out, dk_out, dv_out, gate_out, dq_here, dk_here, dv_here, sem):
    steps = [(dk, dk_here, dk_out), (dv, dv_here, dv_out)]
    for i in range(4):
        rows = pl.ds(i * 64, 64)
        steps.append((dq.at[rows], dq_here.at[rows], dq_out.at[rows]))
    first = [pltpu.make_async_copy(a, b, sem.at[i]) for i, (a, b, _) in enumerate(steps)]
    second = [pltpu.make_async_copy(b, c, sem.at[6 + i]) for i, (_, b, c) in enumerate(steps)]
    for one in first:
        one.start()
    gate_out[0] = gate[0]
    for one, two in zip(first, second):
        one.wait()
        two.start()
    for two in second:
        two.wait()


def per_device(queries, cotangent, image_keys, image_values, attn_gate, block_mask, image_owner):
    shape = jax.ShapeDtypeStruct
    dma = pltpu.SemaphoreType.DMA
    rows = shape((TOK, HEADS * HD), BF16)
    rows_here = pltpu.VMEM((TOK, HEADS * HD), BF16)
    part_a, part_b = pltpu.VMEM((8, RA, HD), BF16), pltpu.VMEM((8, RB, HD), BF16)
    whole_a, whole_b = pltpu.VMEM((SLOTS, RA, HD), BF16), pltpu.VMEM((SLOTS, RB, HD), BF16)
    grad = shape((1, IMG, HD), BF16)
    anywhere = pl.BlockSpec(memory_space=pltpu.HBM)
    results = pl.pallas_call(
        kernel,
        out_shape=[rows, grad, grad, shape((1,), F32)],
        in_specs=[anywhere] * 7,
        out_specs=[anywhere, VM, VM, SM],
        scratch_shapes=[
            pltpu.SMEM((2, SLOTS), jnp.int32),
            pltpu.SMEM((SLOTS,), jnp.int32),
            pltpu.SMEM((1,), F32),
            pltpu.VMEM((8, HD), jnp.int32),
            pltpu.SMEM((8, HD), jnp.int32),
            rows_here,
            rows_here,
            rows_here,
        ]
        + [whole_a, whole_b] * 2
        + [
            pltpu.VMEM((KEYS, 2 * HD), BF16),
            pltpu.VMEM((KEYS, HD), BF16),
            pltpu.VMEM((HD, KEYS), BF16),
            pltpu.VMEM((TOGETHER, KEYS, TOK), F32),
            pltpu.VMEM((HEADS, KEYS, TOK), BF16),
            pltpu.VMEM((HEADS, KEYS, TOK), BF16),
            pltpu.VMEM((READ + 1, IMG, HD), F32),
            pltpu.VMEM((READ + 1, IMG, HD), F32),
        ]
        + [whole_a, whole_b] * 4
        + [part_a, part_b] * 4
        + [pltpu.VMEM((8, TOK), F32), pltpu.VMEM((3, 8, HD), F32), pltpu.VMEM((3, 7, 8, HD), F32)]
        + [dma((11,)), dma((19,)), dma((19,))],
        compiler_params=pltpu.CompilerParams(
            collective_id=0, has_side_effects=True, vmem_limit_bytes=(64 << 20) - (64 << 10)
        ),
    )(block_mask, image_owner, attn_gate, queries, cotangent, image_keys, image_values)
    return pl.pallas_call(
        hand_over,
        out_shape=[rows, grad, grad, shape((1,), F32)],
        in_specs=[anywhere] * 3 + [SM],
        out_specs=[anywhere] * 3 + [SM],
        scratch_shapes=[rows_here, pltpu.VMEM((1, IMG, HD), BF16), pltpu.VMEM((1, IMG, HD), BF16), dma((12,))],
        compiler_params=pltpu.CompilerParams(vmem_limit_bytes=(64 << 20) - (64 << 10)),
    )(*results)


def solution(mesh):
    specs = (P("ctx", "tp"), P("ctx", "tp"), P("ctx", None, "tp"), P("ctx", None, "tp"), P(), P("ctx", None), P())
    outs = (P("ctx", "tp"), P("ctx", None, "tp"), P("ctx", None, "tp"), P())
    return jax.shard_map(per_device, mesh=mesh, in_specs=specs, out_specs=outs, check_vma=False)
```

```python
import functools
import math

import jax
import jax.numpy as jnp
from jax import lax
from jax.experimental import pallas as pl
from jax.experimental.pallas import tpu as pltpu
from jax.sharding import PartitionSpec as P

HD = 128
HEADS = 8
TOK = 256
BLK = 128
IMG = 64
SLOTS = 64
READ = 32
KEYS = READ * IMG
CHUNK = 512
TOGETHER = 4
RA, RB = 16, 48
X, Y, Z = 4, 2, 8
TERMS = 16384 * 8192
SCALE = math.log2(math.e) / math.sqrt(HD)
NT = (((1,), (1,)), ((), ()))
F32 = jnp.float32
BF16 = jnp.bfloat16
MESH = pl.DeviceIdType.MESH
PLANE = ((0, 1), (1, 0), (1, 1), (3, 0), (3, 1), (2, 0), (2, 1))
LINE = (4, 1, 7, 2, 6, 3, 5)
VM = pl.BlockSpec(memory_space=pltpu.VMEM)
SM = pl.BlockSpec(memory_space=pltpu.SMEM)


class Place:
    def __init__(self):
        ctx = lax.axis_index("ctx")
        self.tp = lax.axis_index("tp")
        self.x = lax.rem(ctx, X)
        self.z = lax.rem(ctx // X, Z)
        self.y = ctx // (X * Z)
        self.p = self.y * X + self.x

    def z_at(self, d):
        return lax.rem(self.z + d + Z, Z)

    def p_at(self, dx, dy):
        return lax.rem(self.y + dy, Y) * X + lax.rem(self.x + dx + X, X)

    def z_dev(self, d):
        return ((self.y * Z + self.z_at(d)) * X + self.x, self.tp)

    def p_dev(self, dx, dy):
        y, x = lax.rem(self.y + dy, Y), lax.rem(self.x + dx + X, X)
        return ((y * Z + self.z) * X + x, self.tp)

    def tp_dev(self, d):
        return ((self.y * Z + self.z) * X + self.x, lax.rem(self.tp + d, 8))


def greet(devices):
    barrier = pltpu.get_barrier_semaphore()
    for dev in devices:
        pl.semaphore_signal(barrier, inc=1, device_id=dev, device_id_type=MESH)
    pl.semaphore_wait(barrier, len(devices))


class Wires:
    def __init__(self, send_sem, recv_sem):
        self.send_sem, self.recv_sem, self.groups, self.gone = send_sem, recv_sem, {}, []

    def copy(self, src, dst, dev, group):
        return pltpu.make_async_remote_copy(
            src_ref=src,
            dst_ref=dst,
            send_sem=self.send_sem.at[group],
            recv_sem=self.recv_sem.at[group],
            device_id=dev,
            device_id_type=MESH,
        )

    def send(self, src, dst, dev, group):
        self.copy(src, dst, dev, group).start()

    def arrived(self, whole, dev, group):
        one = self.copy(whole, whole, dev, group)
        one.wait_recv()
        self.groups[group] = one

    def left(self, whole, dev, group):
        self.copy(whole, whole, dev, group).wait_send()
        self.gone.append(group)

    def drain(self):
        for group, one in self.groups.items():
            if group not in self.gone:
                one.wait_send()


def gather_first(me, wires, src, ga, gb, base):
    for d in LINE:
        wires.send(src.at[0, RA:IMG], gb.at[me.p * 8 + me.z], me.z_dev(d), base)
    for dx, dy in PLANE:
        wires.send(src.at[0, 0:RA], ga.at[me.z * 8 + me.p], me.p_dev(dx, dy), base + 1)


def gather_second(me, wires, ga, gb, base):
    wires.arrived(gb.at[pl.ds(0, 7)], me.z_dev(1), base)
    row = gb.at[pl.ds(me.p * 8, 8)]
    for dx, dy in PLANE:
        wires.send(row, row, me.p_dev(dx, dy), base + 2)
    wires.arrived(ga.at[pl.ds(0, 7)], me.z_dev(1), base + 1)
    row = ga.at[pl.ds(me.z * 8, 8)]
    for d in LINE:
        wires.send(row, row, me.z_dev(d), base + 3)


def gather_last(me, wires, ga, gb, base):
    wires.arrived(gb.at[pl.ds(0, 56)], me.z_dev(1), base + 2)
    wires.arrived(ga.at[pl.ds(0, 56)], me.z_dev(1), base + 3)


def head_lanes(h):
    return pl.ds(pl.multiple_of(h * HD, HD), HD)


def find_reads(mask_ref, owner_ref, table):
    down = lax.broadcasted_iota(jnp.int32, (SLOTS, HD), 0)
    across = lax.broadcasted_iota(jnp.int32, (SLOTS, HD), 1)

    def image(i, reads):
        slot = owner_ref[i]
        hit = down == ((slot // X) % Z) * 8 + (slot // (X * Z)) * X + slot % X
        return tuple(jnp.where(hit, mask_ref[b, i], r) for b, r in enumerate(reads))

    def total(where, what):
        return jnp.sum(jnp.where(where, what, 0), axis=0, keepdims=True)

    zero = jnp.zeros((SLOTS, HD), jnp.int32)
    first, second = lax.fori_loop(0, SLOTS, image, (zero, zero))
    read = jnp.minimum(first + second, 1)
    position = jnp.where(total(down == across, read) > 0, total(down < across, read), READ)
    chosen = jnp.broadcast_to(position, (HD, HD)).T[0:SLOTS] == across
    sub = lax.broadcasted_iota(jnp.int32, (8, HD), 0)
    low = jnp.where(sub == 0, total(chosen, down), total(chosen, first))
    high = jnp.where(sub == 2, total(chosen, second), position)
    turned = lax.rem(down, 8) * 8 + down // 8
    table[...] = jnp.where(sub < 2, low, jnp.where(sub < 4, high, total(chosen, turned)))


def mask_columns(table, dst):
    lane = lax.broadcasted_iota(jnp.int32, (IMG, HD), 1)
    for j in range(READ):
        b0 = jnp.where(table[1, j] > 0, 0.0, -1e30)
        b1 = jnp.where(table[2, j] > 0, 0.0, -1e30)
        bias = jnp.where(lane == 0, b0, jnp.where(lane == 1, b1, 0.0))
        dst[j * IMG : (j + 1) * IMG, HD : 2 * HD] = bias.astype(BF16)


def pick_rows(table, a_ref, b_ref, dst):
    for j in range(READ):
        at = j * IMG
        dst[at : at + RA, 0:HD] = a_ref[table[0, j]]
        dst[at + RA : at + IMG, 0:HD] = b_ref[table[4, j]]


def fold(x, op):
    return op(x.reshape(CHUNK // 8, 8, TOK), axis=0)


def add_rows(acc, k, part):
    acc[k // IMG : (k + CHUNK) // IMG] += part.reshape(CHUNK // IMG, IMG, HD)


def softmax_and_values(q_ref, c_ref, kc, s_ref, p_ref, dv_ref):
    lane = lax.broadcasted_iota(jnp.int32, (TOK, HD), 1)
    row = lax.broadcasted_iota(jnp.int32, (TOK, HD), 0)
    block_of = (lane == row // BLK).astype(BF16)
    chunks = range(0, KEYS, CHUNK)

    def some_heads(i, _):
        heads = [i * TOGETHER + j for j in range(TOGETHER)]
        query = [jnp.concatenate([q_ref[:, head_lanes(h)], block_of], axis=1) for h in heads]
        top = [jnp.full((8, TOK), -jnp.inf, F32) for _ in heads]
        for k in chunks:
            for j in range(TOGETHER):
                s = lax.dot_general(kc[k : k + CHUNK, :], query[j], NT, preferred_element_type=F32)
                top[j] = jnp.maximum(top[j], fold(s, jnp.max))
        top = [jnp.max(t, axis=0, keepdims=True) * SCALE for t in top]
        total = [jnp.zeros((8, TOK), F32) for _ in heads]
        for k in chunks:
            for j in range(TOGETHER):
                s = lax.dot_general(kc[k : k + CHUNK, :], query[j], NT, preferred_element_type=F32)
                e = jnp.exp2(s * SCALE - top[j])
                s_ref[j, k : k + CHUNK, :] = e
                total[j] = total[j] + fold(e, jnp.sum)
        inverse = [1.0 / jnp.sum(t, axis=0, keepdims=True) for t in total]
        cot = jnp.concatenate([c_ref[:, head_lanes(h)] for h in heads], axis=0)
        for k in chunks:
            probs = []
            for j, h in enumerate(heads):
                prob = (s_ref[j, k : k + CHUNK, :] * inverse[j]).astype(BF16)
                p_ref[h, k : k + CHUNK, :] = prob
                probs.append(prob)
            add_rows(dv_ref, k, jnp.dot(jnp.concatenate(probs, axis=1), cot, preferred_element_type=F32))
        return 0

    lax.fori_loop(0, HEADS // TOGETHER, some_heads, 0)


def score_and_keys(q_ref, c_ref, vc, s_ref, p_ref, ds_ref, dk_ref, gate_ref):
    chunks = range(0, KEYS, CHUNK)

    def some_heads(i, _):
        heads = [i * TOGETHER + j for j in range(TOGETHER)]
        cot = [c_ref[:, head_lanes(h)] for h in heads]
        delta = [jnp.zeros((8, TOK), F32) for _ in heads]
        for k in chunks:
            for j, h in enumerate(heads):
                dp = lax.dot_general(vc[k : k + CHUNK, :], cot[j], NT, preferred_element_type=F32)
                s_ref[j, k : k + CHUNK, :] = dp
                delta[j] = delta[j] + fold(dp * p_ref[h, k : k + CHUNK, :].astype(F32), jnp.sum)
        gate_ref[...] += sum(delta)
        delta = [jnp.sum(d, axis=0, keepdims=True) for d in delta]
        query = jnp.concatenate([q_ref[:, head_lanes(h)] for h in heads], axis=0)
        for k in chunks:
            grads = []
            for j, h in enumerate(heads):
                prob = p_ref[h, k : k + CHUNK, :].astype(F32)
                ds = (prob * (s_ref[j, k : k + CHUNK, :] - delta[j])).astype(BF16)
                ds_ref[h, k : k + CHUNK, :] = ds
                grads.append(ds)
            add_rows(dk_ref, k, jnp.dot(jnp.concatenate(grads, axis=1), query, preferred_element_type=F32))
        return 0

    lax.fori_loop(0, HEADS // TOGETHER, some_heads, 0)


def queries_grad(kt, ds_ref, dq_ref, scale):
    def head(h, _):
        t = jnp.dot(kt[...], ds_ref[h], preferred_element_type=F32) * scale
        dq_ref[:, head_lanes(h)] = t.T.astype(BF16)
        return 0

    lax.fori_loop(0, HEADS, head, 0)


def reduce_first(me, wires, table, acc, scale, sa, sb, ra, rb, base):
    def fill_b(p):
        for z in range(Z):
            sb[p * 8 + z] = (acc[table[3, z * 8 + p], RA:IMG] * scale).astype(BF16)

    def fill_a(z):
        for p in range(X * Y):
            sa[z * 8 + p] = (acc[table[3, z * 8 + p], 0:RA] * scale).astype(BF16)

    for dx, dy in PLANE:
        there = me.p_at(dx, dy)
        fill_b(there)
        wires.send(sb.at[pl.ds(there * 8, 8)], rb.at[pl.ds(me.p * 8, 8)], me.p_dev(dx, dy), base)
    for d in LINE:
        there = me.z_at(d)
        fill_a(there)
        wires.send(sa.at[pl.ds(there * 8, 8)], ra.at[pl.ds(me.z * 8, 8)], me.z_dev(d), base + 1)
    fill_b(me.p)
    fill_a(me.z)


def reduce_second(me, wires, sa, sb, ra, rb, ta, tb, ua, ub, base):
    wires.arrived(rb.at[pl.ds(0, 56)], me.z_dev(1), base)
    total = sb[pl.ds(me.p * 8, 8)].astype(F32)
    for dx, dy in PLANE:
        total = total + rb[pl.ds(me.p_at(dx, dy) * 8, 8)].astype(F32)
    tb[...] = total.astype(BF16)
    for d in LINE:
        wires.send(tb.at[me.z_at(d)], ub.at[me.z], me.z_dev(d), base + 2)
    wires.arrived(ra.at[pl.ds(0, 56)], me.z_dev(1), base + 1)
    total = sa[pl.ds(me.z * 8, 8)].astype(F32)
    for d in LINE:
        total = total + ra[pl.ds(me.z_at(d) * 8, 8)].astype(F32)
    ta[...] = total.astype(BF16)
    for dx, dy in PLANE:
        wires.send(ta.at[me.p_at(dx, dy)], ua.at[me.p], me.p_dev(dx, dy), base + 3)


def reduce_last(me, wires, ta, tb, ua, ub, out, base):
    wires.arrived(ub.at[pl.ds(0, 7)], me.z_dev(1), base + 2)
    total = tb[me.z].astype(F32)
    for d in LINE:
        total = total + ub[me.z_at(d)].astype(F32)
    out[0, RA:IMG] = total.astype(BF16)
    wires.arrived(ua.at[pl.ds(0, 7)], me.z_dev(1), base + 3)
    total = ta[me.p].astype(F32)
    for dx, dy in PLANE:
        total = total + ua[me.p_at(dx, dy)].astype(F32)
    out[0, 0:RA] = total.astype(BF16)


def gate_step(wires, own, box, devices, group):
    for i, dev in enumerate(devices):
        wires.send(own, box.at[i], dev, group)

    def finish():
        wires.arrived(box, devices[0], group)
        return own[...] + jnp.sum(box[...], axis=0)

    return finish


def kernel(
    mask_in, owner_in, gate_in, q_in, c_in, k_in, v_in, dq_out, dk_out, dv_out, gate_out,
    mask_ref, owner_ref, gate_ref, table_v, table, q_ref, c_ref, dq_ref,
    ka, kb, va, vb, kc, vc, kt, s_ref, p_ref, ds_ref, dk_ref, dv_ref,
    dka, dkb, dva, dvb, rka, rkb, rva, rvb, tka, tkb, tva, tvb, uka, ukb, uva, uvb,
    gate_rows, gate_own, gate_box, local_sem, send_sem, recv_sem,
):
    me = Place()
    along_z = [me.z_dev(d) for d in LINE]
    in_plane = [me.p_dev(*d) for d in PLANE]
    along_tp = [me.tp_dev(d) for d in range(1, 8)]
    here_a, here_b = me.z * 8 + me.p, me.p * 8 + me.z
    inputs = [
        pltpu.make_async_copy(src, dst, local_sem.at[i])
        for i, (src, dst) in enumerate(
            (
                (k_in.at[0, 0:RA], ka.at[here_a]),
                (k_in.at[0, RA:IMG], kb.at[here_b]),
                (v_in.at[0, 0:RA], va.at[here_a]),
                (v_in.at[0, RA:IMG], vb.at[here_b]),
                (mask_in, mask_ref),
                (owner_in, owner_ref),
                (gate_in, gate_ref),
                (q_in, q_ref),
                (c_in, c_ref),
            )
        )
    ]
    for one in inputs:
        one.start()
    greet(along_z + in_plane + along_tp)
    wires = Wires(send_sem, recv_sem)
    gather_first(me, wires, k_in, ka, kb, 0)
    gather_first(me, wires, v_in, va, vb, 4)
    for one in inputs:
        one.wait()
    gate = jnp.tanh(jnp.full((1, HD), gate_ref[0], F32))
    find_reads(mask_ref, owner_ref, table_v)
    put = pltpu.make_async_copy(table_v, table, local_sem.at[9])
    put.start()
    dk_ref[...] = jnp.zeros_like(dk_ref)
    dv_ref[...] = jnp.zeros_like(dv_ref)
    gate_rows[...] = jnp.zeros_like(gate_rows)
    put.wait()
    gather_second(me, wires, ka, kb, 0)
    mask_columns(table, kc)
    wires.left(kb.at[pl.ds(0, 56)], me.z_dev(1), 2)
    wires.left(ka.at[pl.ds(0, 56)], me.z_dev(1), 3)
    gather_second(me, wires, va, vb, 4)
    gather_last(me, wires, ka, kb, 0)
    pick_rows(table, ka, kb, kc)
    softmax_and_values(q_ref, c_ref, kc, s_ref, p_ref, dv_ref)
    reduce_first(me, wires, table, dv_ref, gate, dva, dvb, rva, rvb, 8)
    gather_last(me, wires, va, vb, 4)
    pick_rows(table, va, vb, vc)
    score_and_keys(q_ref, c_ref, vc, s_ref, p_ref, ds_ref, dk_ref, gate_rows)
    gate_own[0] = gate_rows[:, 0:HD] + gate_rows[:, HD : 2 * HD]
    step = gate_step(wires, gate_own.at[0], gate_box.at[0], along_z, 16)
    scale = gate * (1.0 / math.sqrt(HD))
    reduce_first(me, wires, table, dk_ref, scale, dka, dkb, rka, rkb, 12)
    kt[...] = kc[:, 0:HD].T
    queries_grad(kt, ds_ref, dq_ref, jnp.concatenate([scale, scale], axis=1))
    back = pltpu.make_async_copy(dq_ref, dq_out, local_sem.at[10])
    back.start()
    reduce_second(me, wires, dva, dvb, rva, rvb, tva, tvb, uva, uvb, 8)
    gate_own[1] = step()
    step = gate_step(wires, gate_own.at[1], gate_box.at[1], in_plane, 17)
    reduce_last(me, wires, tva, tvb, uva, uvb, dv_out, 8)
    gate_own[2] = step()
    step = gate_step(wires, gate_own.at[2], gate_box.at[2], along_tp, 18)
    reduce_second(me, wires, dka, dkb, rka, rkb, tka, tkb, uka, ukb, 12)
    reduce_last(me, wires, tka, tkb, uka, ukb, dk_out, 12)
    gate = jnp.tanh(jnp.full((8, HD), gate_ref[0], F32))
    gate_out[0] = jnp.sum((1.0 - gate * gate) * step()) * (1.0 / math.sqrt(TERMS))
    back.wait()
    wires.drain()


def hand_over(dq, dk, dv, gate, dq_out, dk_out, dv_out, gate_out, dq_here, dk_here, dv_here, sem):
    steps = [(dk, dk_here, dk_out), (dv, dv_here, dv_out)]
    for i in range(4):
        rows = pl.ds(i * 64, 64)
        steps.append((dq.at[rows], dq_here.at[rows], dq_out.at[rows]))
    first = [pltpu.make_async_copy(a, b, sem.at[i]) for i, (a, b, _) in enumerate(steps)]
    second = [pltpu.make_async_copy(b, c, sem.at[6 + i]) for i, (_, b, c) in enumerate(steps)]
    for one in first:
        one.start()
    gate_out[0] = gate[0]
    for one, two in zip(first, second):
        one.wait()
        two.start()
    for two in second:
        two.wait()


def per_device(queries, cotangent, image_keys, image_values, attn_gate, block_mask, image_owner):
    shape = jax.ShapeDtypeStruct
    dma = pltpu.SemaphoreType.DMA
    rows = shape((TOK, HEADS * HD), BF16)
    rows_here = pltpu.VMEM((TOK, HEADS * HD), BF16)
    part_a, part_b = pltpu.VMEM((8, RA, HD), BF16), pltpu.VMEM((8, RB, HD), BF16)
    whole_a, whole_b = pltpu.VMEM((SLOTS, RA, HD), BF16), pltpu.VMEM((SLOTS, RB, HD), BF16)
    grad = shape((1, IMG, HD), BF16)
    anywhere = pl.BlockSpec(memory_space=pltpu.HBM)
    results = pl.pallas_call(
        kernel,
        out_shape=[rows, grad, grad, shape((1,), F32)],
        in_specs=[anywhere] * 7,
        out_specs=[anywhere, VM, VM, SM],
        scratch_shapes=[
            pltpu.SMEM((2, SLOTS), jnp.int32),
            pltpu.SMEM((SLOTS,), jnp.int32),
            pltpu.SMEM((1,), F32),
            pltpu.VMEM((8, HD), jnp.int32),
            pltpu.SMEM((8, HD), jnp.int32),
            rows_here,
            rows_here,
            rows_here,
        ]
        + [whole_a, whole_b] * 2
        + [
            pltpu.VMEM((KEYS, 2 * HD), BF16),
            pltpu.VMEM((KEYS, HD), BF16),
            pltpu.VMEM((HD, KEYS), BF16),
            pltpu.VMEM((TOGETHER, KEYS, TOK), F32),
            pltpu.VMEM((HEADS, KEYS, TOK), BF16),
            pltpu.VMEM((HEADS, KEYS, TOK), BF16),
            pltpu.VMEM((READ + 1, IMG, HD), F32),
            pltpu.VMEM((READ + 1, IMG, HD), F32),
        ]
        + [whole_a, whole_b] * 4
        + [part_a, part_b] * 4
        + [pltpu.VMEM((8, TOK), F32), pltpu.VMEM((3, 8, HD), F32), pltpu.VMEM((3, 7, 8, HD), F32)]
        + [dma((11,)), dma((19,)), dma((19,))],
        compiler_params=pltpu.CompilerParams(
            collective_id=0, has_side_effects=True, vmem_limit_bytes=(64 << 20) - (64 << 10)
        ),
    )(block_mask, image_owner, attn_gate, queries, cotangent, image_keys, image_values)
    return pl.pallas_call(
        hand_over,
        out_shape=[rows, grad, grad, shape((1,), F32)],
        in_specs=[anywhere] * 3 + [SM],
        out_specs=[anywhere] * 3 + [SM],
        scratch_shapes=[rows_here, pltpu.VMEM((1, IMG, HD), BF16), pltpu.VMEM((1, IMG, HD), BF16), dma((12,))],
        compiler_params=pltpu.CompilerParams(vmem_limit_bytes=(64 << 20) - (64 << 10)),
    )(*results)


def solution(mesh):
    specs = (P("ctx", "tp"), P("ctx", "tp"), P("ctx", None, "tp"), P("ctx", None, "tp"), P(), P("ctx", None), P())
    outs = (P("ctx", "tp"), P("ctx", None, "tp"), P("ctx", None, "tp"), P())
    return jax.shard_map(per_device, mesh=mesh, in_specs=specs, out_specs=outs, check_vma=False)
```

```python
import functools
import math

import jax
import jax.numpy as jnp
from jax import lax
from jax.experimental import pallas as pl
from jax.experimental.pallas import tpu as pltpu
from jax.sharding import PartitionSpec as P

HD = 128
HEADS = 8
TOK = 256
BLK = 128
IMG = 64
SLOTS = 64
READ = 32
KEYS = READ * IMG
CHUNK = 512
TOGETHER = 4
RA, RB = 16, 48
X, Y, Z = 4, 2, 8
TERMS = 16384 * 8192
SCALE = math.log2(math.e) / math.sqrt(HD)
NT = (((1,), (1,)), ((), ()))
F32 = jnp.float32
BF16 = jnp.bfloat16
MESH = pl.DeviceIdType.MESH
PLANE = [(dx, dy) for dy in range(Y) for dx in range(X) if dx + dy]
VM = pl.BlockSpec(memory_space=pltpu.VMEM)
SM = pl.BlockSpec(memory_space=pltpu.SMEM)


class Place:
    def __init__(self):
        ctx = lax.axis_index("ctx")
        self.tp = lax.axis_index("tp")
        self.x = lax.rem(ctx, X)
        self.z = lax.rem(ctx // X, Z)
        self.y = ctx // (X * Z)
        self.p = self.y * X + self.x

    def z_at(self, d):
        return lax.rem(self.z + d + Z, Z)

    def p_at(self, dx, dy):
        return lax.rem(self.y + dy, Y) * X + lax.rem(self.x + dx + X, X)

    def z_dev(self, d):
        return ((self.y * Z + self.z_at(d)) * X + self.x, self.tp)

    def p_dev(self, dx, dy):
        y, x = lax.rem(self.y + dy, Y), lax.rem(self.x + dx + X, X)
        return ((y * Z + self.z) * X + x, self.tp)

    def tp_dev(self, d):
        return ((self.y * Z + self.z) * X + self.x, lax.rem(self.tp + d, 8))


def greet(devices):
    barrier = pltpu.get_barrier_semaphore()
    for dev in devices:
        pl.semaphore_signal(barrier, inc=1, device_id=dev, device_id_type=MESH)
    pl.semaphore_wait(barrier, len(devices))


class Wires:
    def __init__(self, send_sem, recv_sem):
        self.send_sem, self.recv_sem, self.groups, self.gone = send_sem, recv_sem, {}, []

    def copy(self, src, dst, dev, group):
        return pltpu.make_async_remote_copy(
            src_ref=src,
            dst_ref=dst,
            send_sem=self.send_sem.at[group],
            recv_sem=self.recv_sem.at[group],
            device_id=dev,
            device_id_type=MESH,
        )

    def send(self, src, dst, dev, group):
        self.copy(src, dst, dev, group).start()

    def arrived(self, whole, dev, group):
        one = self.copy(whole, whole, dev, group)
        one.wait_recv()
        self.groups[group] = one

    def left(self, whole, dev, group):
        self.copy(whole, whole, dev, group).wait_send()
        self.gone.append(group)

    def drain(self):
        for group, one in self.groups.items():
            if group not in self.gone:
                one.wait_send()


def gather_first(me, wires, ga, gb, base):
    for d in range(1, Z):
        spot = gb.at[me.p * 8 + me.z]
        wires.send(spot, spot, me.z_dev(d), base)
    for dx, dy in PLANE:
        spot = ga.at[me.z * 8 + me.p]
        wires.send(spot, spot, me.p_dev(dx, dy), base + 1)


def gather_second(me, wires, ga, gb, base):
    wires.arrived(gb.at[pl.ds(0, 7)], me.z_dev(1), base)
    row = gb.at[pl.ds(me.p * 8, 8)]
    for dx, dy in PLANE:
        wires.send(row, row, me.p_dev(dx, dy), base + 2)
    wires.arrived(ga.at[pl.ds(0, 7)], me.z_dev(1), base + 1)
    row = ga.at[pl.ds(me.z * 8, 8)]
    for d in range(1, Z):
        wires.send(row, row, me.z_dev(d), base + 3)


def gather_last(me, wires, ga, gb, base):
    wires.arrived(gb.at[pl.ds(0, 56)], me.z_dev(1), base + 2)
    wires.arrived(ga.at[pl.ds(0, 56)], me.z_dev(1), base + 3)


def head_lanes(h):
    return pl.ds(pl.multiple_of(h * HD, HD), HD)


def find_reads(mask_ref, owner_ref, table):
    down = lax.broadcasted_iota(jnp.int32, (SLOTS, HD), 0)
    across = lax.broadcasted_iota(jnp.int32, (SLOTS, HD), 1)

    def image(i, reads):
        slot = owner_ref[i]
        hit = down == ((slot // X) % Z) * 8 + (slot // (X * Z)) * X + slot % X
        return tuple(jnp.where(hit, mask_ref[b, i], r) for b, r in enumerate(reads))

    def total(where, what):
        return jnp.sum(jnp.where(where, what, 0), axis=0, keepdims=True)

    zero = jnp.zeros((SLOTS, HD), jnp.int32)
    first, second = lax.fori_loop(0, SLOTS, image, (zero, zero))
    read = jnp.minimum(first + second, 1)
    position = jnp.where(total(down == across, read) > 0, total(down < across, read), READ)
    chosen = jnp.broadcast_to(position, (HD, HD)).T[0:SLOTS] == across
    sub = lax.broadcasted_iota(jnp.int32, (8, HD), 0)
    low = jnp.where(sub == 0, total(chosen, down), total(chosen, first))
    high = jnp.where(sub == 2, total(chosen, second), position)
    turned = lax.rem(down, 8) * 8 + down // 8
    table[...] = jnp.where(sub < 2, low, jnp.where(sub < 4, high, total(chosen, turned)))


def mask_columns(table, dst):
    lane = lax.broadcasted_iota(jnp.int32, (IMG, HD), 1)
    for j in range(READ):
        b0 = jnp.where(table[1, j] > 0, 0.0, -1e30)
        b1 = jnp.where(table[2, j] > 0, 0.0, -1e30)
        bias = jnp.where(lane == 0, b0, jnp.where(lane == 1, b1, 0.0))
        dst[j * IMG : (j + 1) * IMG, HD : 2 * HD] = bias.astype(BF16)


def pick_rows(table, a_ref, b_ref, dst):
    for j in range(READ):
        at = j * IMG
        dst[at : at + RA, 0:HD] = a_ref[table[0, j]]
        dst[at + RA : at + IMG, 0:HD] = b_ref[table[4, j]]


def fold(x, op):
    return op(x.reshape(CHUNK // 8, 8, TOK), axis=0)


def add_rows(acc, k, part):
    acc[k // IMG : (k + CHUNK) // IMG] += part.reshape(CHUNK // IMG, IMG, HD)


def softmax_and_values(q_ref, c_ref, kc, s_ref, p_ref, dv_ref):
    lane = lax.broadcasted_iota(jnp.int32, (TOK, HD), 1)
    row = lax.broadcasted_iota(jnp.int32, (TOK, HD), 0)
    block_of = (lane == row // BLK).astype(BF16)
    chunks = range(0, KEYS, CHUNK)

    def some_heads(i, _):
        heads = [i * TOGETHER + j for j in range(TOGETHER)]
        query = [jnp.concatenate([q_ref[:, head_lanes(h)], block_of], axis=1) for h in heads]
        top = [jnp.full((8, TOK), -jnp.inf, F32) for _ in heads]
        for k in chunks:
            for j in range(TOGETHER):
                s = lax.dot_general(kc[k : k + CHUNK, :], query[j], NT, preferred_element_type=F32)
                top[j] = jnp.maximum(top[j], fold(s, jnp.max))
        top = [jnp.max(t, axis=0, keepdims=True) * SCALE for t in top]
        total = [jnp.zeros((8, TOK), F32) for _ in heads]
        for k in chunks:
            for j in range(TOGETHER):
                s = lax.dot_general(kc[k : k + CHUNK, :], query[j], NT, preferred_element_type=F32)
                e = jnp.exp2(s * SCALE - top[j])
                s_ref[j, k : k + CHUNK, :] = e
                total[j] = total[j] + fold(e, jnp.sum)
        inverse = [1.0 / jnp.sum(t, axis=0, keepdims=True) for t in total]
        cot = jnp.concatenate([c_ref[:, head_lanes(h)] for h in heads], axis=0)
        for k in chunks:
            probs = []
            for j, h in enumerate(heads):
                prob = (s_ref[j, k : k + CHUNK, :] * inverse[j]).astype(BF16)
                p_ref[h, k : k + CHUNK, :] = prob
                probs.append(prob)
            add_rows(dv_ref, k, jnp.dot(jnp.concatenate(probs, axis=1), cot, preferred_element_type=F32))
        return 0

    lax.fori_loop(0, HEADS // TOGETHER, some_heads, 0)


def score_and_keys(q_ref, c_ref, vc, s_ref, p_ref, ds_ref, dk_ref, gate_ref):
    chunks = range(0, KEYS, CHUNK)

    def some_heads(i, _):
        heads = [i * TOGETHER + j for j in range(TOGETHER)]
        cot = [c_ref[:, head_lanes(h)] for h in heads]
        delta = [jnp.zeros((8, TOK), F32) for _ in heads]
        for k in chunks:
            for j, h in enumerate(heads):
                dp = lax.dot_general(vc[k : k + CHUNK, :], cot[j], NT, preferred_element_type=F32)
                s_ref[j, k : k + CHUNK, :] = dp
                delta[j] = delta[j] + fold(dp * p_ref[h, k : k + CHUNK, :].astype(F32), jnp.sum)
        gate_ref[...] += sum(delta)
        delta = [jnp.sum(d, axis=0, keepdims=True) for d in delta]
        query = jnp.concatenate([q_ref[:, head_lanes(h)] for h in heads], axis=0)
        for k in chunks:
            grads = []
            for j, h in enumerate(heads):
                prob = p_ref[h, k : k + CHUNK, :].astype(F32)
                ds = (prob * (s_ref[j, k : k + CHUNK, :] - delta[j])).astype(BF16)
                ds_ref[h, k : k + CHUNK, :] = ds
                grads.append(ds)
            add_rows(dk_ref, k, jnp.dot(jnp.concatenate(grads, axis=1), query, preferred_element_type=F32))
        return 0

    lax.fori_loop(0, HEADS // TOGETHER, some_heads, 0)


def queries_grad(kt, ds_ref, dq_ref, scale):
    def head(h, _):
        t = jnp.dot(kt[...], ds_ref[h], preferred_element_type=F32) * scale
        dq_ref[:, head_lanes(h)] = t.T.astype(BF16)
        return 0

    lax.fori_loop(0, HEADS, head, 0)


def reduce_first(me, wires, table, acc, scale, sa, sb, ra, rb, base):
    def fill_b(p):
        for z in range(Z):
            sb[p * 8 + z] = (acc[table[3, z * 8 + p], RA:IMG] * scale).astype(BF16)

    def fill_a(z):
        for p in range(X * Y):
            sa[z * 8 + p] = (acc[table[3, z * 8 + p], 0:RA] * scale).astype(BF16)

    for dx, dy in PLANE:
        there = me.p_at(dx, dy)
        fill_b(there)
        wires.send(sb.at[pl.ds(there * 8, 8)], rb.at[pl.ds(me.p * 8, 8)], me.p_dev(dx, dy), base)
    for d in range(1, Z):
        there = me.z_at(d)
        fill_a(there)
        wires.send(sa.at[pl.ds(there * 8, 8)], ra.at[pl.ds(me.z * 8, 8)], me.z_dev(d), base + 1)
    fill_b(me.p)
    fill_a(me.z)


def reduce_second(me, wires, sa, sb, ra, rb, ta, tb, ua, ub, base):
    wires.arrived(rb.at[pl.ds(0, 56)], me.z_dev(1), base)
    total = sb[pl.ds(me.p * 8, 8)].astype(F32)
    for dx, dy in PLANE:
        total = total + rb[pl.ds(me.p_at(dx, dy) * 8, 8)].astype(F32)
    tb[...] = total.astype(BF16)
    for d in range(1, Z):
        wires.send(tb.at[me.z_at(d)], ub.at[me.z], me.z_dev(d), base + 2)
    wires.arrived(ra.at[pl.ds(0, 56)], me.z_dev(1), base + 1)
    total = sa[pl.ds(me.z * 8, 8)].astype(F32)
    for d in range(1, Z):
        total = total + ra[pl.ds(me.z_at(d) * 8, 8)].astype(F32)
    ta[...] = total.astype(BF16)
    for dx, dy in PLANE:
        wires.send(ta.at[me.p_at(dx, dy)], ua.at[me.p], me.p_dev(dx, dy), base + 3)


def reduce_last(me, wires, ta, tb, ua, ub, out, base):
    wires.arrived(ub.at[pl.ds(0, 7)], me.z_dev(1), base + 2)
    total = tb[me.z].astype(F32)
    for d in range(1, Z):
        total = total + ub[me.z_at(d)].astype(F32)
    out[0, RA:IMG] = total.astype(BF16)
    wires.arrived(ua.at[pl.ds(0, 7)], me.z_dev(1), base + 3)
    total = ta[me.p].astype(F32)
    for dx, dy in PLANE:
        total = total + ua[me.p_at(dx, dy)].astype(F32)
    out[0, 0:RA] = total.astype(BF16)


def gate_step(wires, own, box, devices, group):
    for i, dev in enumerate(devices):
        wires.send(own, box.at[i], dev, group)

    def finish():
        wires.arrived(box, devices[0], group)
        return own[...] + jnp.sum(box[...], axis=0)

    return finish


def kernel(
    mask_in, owner_in, gate_in, q_in, c_in, k_in, v_in, dq_out, dk_out, dv_out, gate_out,
    mask_ref, owner_ref, gate_ref, table_v, table, q_ref, c_ref, dq_ref,
    ka, kb, va, vb, kc, vc, kt, s_ref, p_ref, ds_ref, dk_ref, dv_ref,
    dka, dkb, dva, dvb, rka, rkb, rva, rvb, tka, tkb, tva, tvb, uka, ukb, uva, uvb,
    gate_rows, gate_own, gate_box, local_sem, send_sem, recv_sem,
):
    me = Place()
    along_z = [me.z_dev(d) for d in range(1, Z)]
    in_plane = [me.p_dev(*d) for d in PLANE]
    along_tp = [me.tp_dev(d) for d in range(1, 8)]
    here_a, here_b = me.z * 8 + me.p, me.p * 8 + me.z
    inputs = [
        pltpu.make_async_copy(src, dst, local_sem.at[i])
        for i, (src, dst) in enumerate(
            (
                (k_in.at[0, 0:RA], ka.at[here_a]),
                (k_in.at[0, RA:IMG], kb.at[here_b]),
                (v_in.at[0, 0:RA], va.at[here_a]),
                (v_in.at[0, RA:IMG], vb.at[here_b]),
                (mask_in, mask_ref),
                (owner_in, owner_ref),
                (gate_in, gate_ref),
                (q_in, q_ref),
                (c_in, c_ref),
            )
        )
    ]
    for one in inputs:
        one.start()
    greet(along_z + in_plane + along_tp)
    wires = Wires(send_sem, recv_sem)
    for one in inputs[:4]:
        one.wait()
    gather_first(me, wires, ka, kb, 0)
    gather_first(me, wires, va, vb, 4)
    for one in inputs[4:]:
        one.wait()
    gate = jnp.tanh(jnp.full((1, HD), gate_ref[0], F32))
    find_reads(mask_ref, owner_ref, table_v)
    put = pltpu.make_async_copy(table_v, table, local_sem.at[9])
    put.start()
    dk_ref[...] = jnp.zeros_like(dk_ref)
    dv_ref[...] = jnp.zeros_like(dv_ref)
    gate_rows[...] = jnp.zeros_like(gate_rows)
    put.wait()
    gather_second(me, wires, ka, kb, 0)
    mask_columns(table, kc)
    wires.left(kb.at[pl.ds(0, 56)], me.z_dev(1), 2)
    wires.left(ka.at[pl.ds(0, 56)], me.z_dev(1), 3)
    gather_second(me, wires, va, vb, 4)
    gather_last(me, wires, ka, kb, 0)
    pick_rows(table, ka, kb, kc)
    softmax_and_values(q_ref, c_ref, kc, s_ref, p_ref, dv_ref)
    reduce_first(me, wires, table, dv_ref, gate, dva, dvb, rva, rvb, 8)
    gather_last(me, wires, va, vb, 4)
    pick_rows(table, va, vb, vc)
    score_and_keys(q_ref, c_ref, vc, s_ref, p_ref, ds_ref, dk_ref, gate_rows)
    gate_own[0] = gate_rows[:, 0:HD] + gate_rows[:, HD : 2 * HD]
    step = gate_step(wires, gate_own.at[0], gate_box.at[0], along_z, 16)
    scale = gate * (1.0 / math.sqrt(HD))
    reduce_first(me, wires, table, dk_ref, scale, dka, dkb, rka, rkb, 12)
    kt[...] = kc[:, 0:HD].T
    queries_grad(kt, ds_ref, dq_ref, jnp.concatenate([scale, scale], axis=1))
    back = pltpu.make_async_copy(dq_ref, dq_out, local_sem.at[10])
    back.start()
    reduce_second(me, wires, dva, dvb, rva, rvb, tva, tvb, uva, uvb, 8)
    gate_own[1] = step()
    step = gate_step(wires, gate_own.at[1], gate_box.at[1], in_plane, 17)
    reduce_last(me, wires, tva, tvb, uva, uvb, dv_out, 8)
    gate_own[2] = step()
    step = gate_step(wires, gate_own.at[2], gate_box.at[2], along_tp, 18)
    reduce_second(me, wires, dka, dkb, rka, rkb, tka, tkb, uka, ukb, 12)
    reduce_last(me, wires, tka, tkb, uka, ukb, dk_out, 12)
    gate = jnp.tanh(jnp.full((8, HD), gate_ref[0], F32))
    gate_out[0] = jnp.sum((1.0 - gate * gate) * step()) * (1.0 / math.sqrt(TERMS))
    back.wait()
    wires.drain()


def hand_over(dq, dk, dv, gate, dq_out, dk_out, dv_out, gate_out, dq_here, dk_here, dv_here, sem):
    steps = [(dk, dk_here, dk_out), (dv, dv_here, dv_out)]
    for i in range(4):
        rows = pl.ds(i * 64, 64)
        steps.append((dq.at[rows], dq_here.at[rows], dq_out.at[rows]))
    first = [pltpu.make_async_copy(a, b, sem.at[i]) for i, (a, b, _) in enumerate(steps)]
    second = [pltpu.make_async_copy(b, c, sem.at[6 + i]) for i, (_, b, c) in enumerate(steps)]
    for one in first:
        one.start()
    gate_out[0] = gate[0]
    for one, two in zip(first, second):
        one.wait()
        two.start()
    for two in second:
        two.wait()


def per_device(queries, cotangent, image_keys, image_values, attn_gate, block_mask, image_owner):
    shape = jax.ShapeDtypeStruct
    dma = pltpu.SemaphoreType.DMA
    rows = shape((TOK, HEADS * HD), BF16)
    rows_here = pltpu.VMEM((TOK, HEADS * HD), BF16)
    part_a, part_b = pltpu.VMEM((8, RA, HD), BF16), pltpu.VMEM((8, RB, HD), BF16)
    whole_a, whole_b = pltpu.VMEM((SLOTS, RA, HD), BF16), pltpu.VMEM((SLOTS, RB, HD), BF16)
    grad = shape((1, IMG, HD), BF16)
    anywhere = pl.BlockSpec(memory_space=pltpu.HBM)
    results = pl.pallas_call(
        kernel,
        out_shape=[rows, grad, grad, shape((1,), F32)],
        in_specs=[anywhere] * 7,
        out_specs=[anywhere, VM, VM, SM],
        scratch_shapes=[
            pltpu.SMEM((2, SLOTS), jnp.int32),
            pltpu.SMEM((SLOTS,), jnp.int32),
            pltpu.SMEM((1,), F32),
            pltpu.VMEM((8, HD), jnp.int32),
            pltpu.SMEM((8, HD), jnp.int32),
            rows_here,
            rows_here,
            rows_here,
        ]
        + [whole_a, whole_b] * 2
        + [
            pltpu.VMEM((KEYS, 2 * HD), BF16),
            pltpu.VMEM((KEYS, HD), BF16),
            pltpu.VMEM((HD, KEYS), BF16),
            pltpu.VMEM((TOGETHER, KEYS, TOK), F32),
            pltpu.VMEM((HEADS, KEYS, TOK), BF16),
            pltpu.VMEM((HEADS, KEYS, TOK), BF16),
            pltpu.VMEM((READ + 1, IMG, HD), F32),
            pltpu.VMEM((READ + 1, IMG, HD), F32),
        ]
        + [whole_a, whole_b] * 4
        + [part_a, part_b] * 4
        + [pltpu.VMEM((8, TOK), F32), pltpu.VMEM((3, 8, HD), F32), pltpu.VMEM((3, 7, 8, HD), F32)]
        + [dma((11,)), dma((19,)), dma((19,))],
        compiler_params=pltpu.CompilerParams(
            collective_id=0, has_side_effects=True, vmem_limit_bytes=(64 << 20) - (64 << 10)
        ),
    )(block_mask, image_owner, attn_gate, queries, cotangent, image_keys, image_values)
    return pl.pallas_call(
        hand_over,
        out_shape=[rows, grad, grad, shape((1,), F32)],
        in_specs=[anywhere] * 3 + [SM],
        out_specs=[anywhere] * 3 + [SM],
        scratch_shapes=[rows_here, pltpu.VMEM((1, IMG, HD), BF16), pltpu.VMEM((1, IMG, HD), BF16), dma((12,))],
        compiler_params=pltpu.CompilerParams(vmem_limit_bytes=(64 << 20) - (64 << 10)),
    )(*results)


def solution(mesh):
    specs = (P("ctx", "tp"), P("ctx", "tp"), P("ctx", None, "tp"), P("ctx", None, "tp"), P(), P("ctx", None), P())
    outs = (P("ctx", "tp"), P("ctx", None, "tp"), P("ctx", None, "tp"), P())
    return jax.shard_map(per_device, mesh=mesh, in_specs=specs, out_specs=outs, check_vma=False)
```
